32 devices in a mesh: tm: 8 (over z, x), fsdp: 4 (over y, core).
Axes of the slice: x: 2, y: 2, z: 4, core: 2. Of those that a mesh axis runs over, the one named last changes fastest.
Arguments:
- latents: bfloat16 [8192, 3072], P(('tm', 'fsdp')), may hold values from -6 to 6
- projected: bfloat16 [8192, 3, 512], P(('tm', 'fsdp')), may hold values from -20 to 20
- out_weight: bfloat16 [512, 3072], P(None, 'fsdp'), may hold values from -0.5 to 0.5
- gate_table: float32 [40, 3072], replicated, may hold values from 0.25 to 2
- timesteps: int32 [32], P('tm'), may hold values from 0 to 39
Outputs:
- updated: bfloat16 [8192, 3072], P(('tm', 'fsdp'))
The draws below stay inside these ranges and needn't reach their ends.
All inputs are finite; a program needn't handle non-finite values.
Results may differ from the reference program's by a relative error of at most 0.0085.
Values may be sent and summed in bfloat16 or wider, within the bound.
A program may use at most 64 MiB of HBM per device.

```python
import math
import jax
import jax.numpy as jnp
from jax import lax

D = 3072
HEAD_DIM = 128
STEPS = 40
FRAME_TOK = 256
HEADS = 4
INNER = 512
FRAMES = 32
TOKENS = 8192


def draw_projected(key, part):
    inner_width = HEADS * HEAD_DIM
    lanes = jnp.array([2.0, 1.0, 1.0], jnp.float32).reshape(1, 3, 1)
    sample = jnp.clip(jax.random.normal(key, (TOKENS, 3, inner_width), jnp.float32), -6.0, 6.0)
    sample = sample * lanes
    signs = jnp.where(jax.random.bernoulli(jax.random.fold_in(key, 11), 0.5, (TOKENS, inner_width)), 1.0, -1.0)
    earlier_signs = jnp.roll(signs, 1, axis=0)
    position = jnp.arange(TOKENS, dtype=jnp.int32)
    within = position % FRAME_TOK
    strength = jnp.array([9.0, 14.0, 20.0], jnp.float32)[position // FRAME_TOK % 3][:, None]
    anchor = (within == 5)[:, None]
    partner = (within == 6)[:, None]
    lifted = 1.0 + 2.0 / (strength * math.sqrt(HEAD_DIM))
    query_part = jnp.where(anchor, strength * signs, sample[:, 0])
    key_part = jnp.where(anchor, signs, jnp.where(partner, earlier_signs * lifted, sample[:, 1]))
    return jnp.stack([query_part, key_part, sample[:, 2]], axis=1).astype(jnp.bfloat16)


def touch_ends(values, rng, low, top_value):
    dims = values.shape
    index_at = [jax.random.randint(jax.random.fold_in(rng, axis), (), 0, dims[axis]) for axis in range(len(dims))]
    values = values.at[tuple(index_at)].set(low)
    longest = dims.index(max(dims))
    index_at[longest] = (index_at[longest] + 1) % dims[longest]
    return values.at[tuple(index_at)].set(top_value)


def steps_of(key, extent, pieces, low, top_value):
    def one(dim, parts):
        draws = jax.random.uniform(jax.random.fold_in(jax.random.fold_in(key, 6), dim), (parts,), jnp.float32, low / len(pieces), top_value / len(pieces))
        return jnp.repeat(jnp.exp(draws), extent[dim] // parts).reshape((-1,) + (1,) * (len(extent) - dim - 1))

    factor_of = one(*pieces[0])
    for cut in pieces[1:]:
        factor_of = factor_of * one(*cut)
    return factor_of


def normal_values(rng, extent, scale, reach, cuts=(), kind=jnp.bfloat16):
    gain = steps_of(rng, extent, cuts, -0.22, 0.18) if cuts else 1.0
    entries = jax.random.normal(rng, extent, jnp.float32) * scale * gain
    return jnp.minimum(jnp.maximum(entries, -reach), reach).astype(kind)


def setup_inputs(seed: int = 0) -> dict:
    streams_of = jax.random.split(jax.random.key(seed), 6)
    return {
        "latents": normal_values(streams_of[0], (TOKENS, D), 1.0, 6.0, ((0, 32),)),
        "projected": draw_projected(jax.random.fold_in(streams_of[5], 71), 0),
        "out_weight": normal_values(streams_of[2], (INNER, D), HEAD_DIM ** -0.5, 0.5, ((1, 4),)),
        "gate_table": jnp.clip(jax.random.uniform(streams_of[3], (STEPS, D), jnp.float32, 0.25, 2.0), 0.25, 2.0),
        "timesteps": touch_ends(jax.random.randint(streams_of[4], (FRAMES,), 0, STEPS), jax.random.fold_in(streams_of[4], 1), 0, STEPS - 1).astype(jnp.int32),
    }


def reference(latents, projected, out_weight, gate_table, timesteps):
    frame_count = timesteps.shape[0]
    head_count = projected.shape[2] // HEAD_DIM
    grouped = projected.reshape(frame_count, FRAME_TOK, 3, head_count, HEAD_DIM)
    padded = jnp.concatenate([jnp.zeros((3, FRAME_TOK, 3, head_count, HEAD_DIM), projected.dtype), grouped], axis=0)
    score_scale = HEAD_DIM ** -0.5
    key_frame = jnp.arange(4 * FRAME_TOK, dtype=jnp.int32) // FRAME_TOK
    residual = latents.reshape(frame_count, FRAME_TOK, latents.shape[1])

    def one_frame(frame_index):
        window = lax.dynamic_slice_in_dim(padded, frame_index, 4, 0)
        queries = window[3, :, 0].astype(jnp.float32)
        key_rows = window[:, :, 1].reshape(4 * FRAME_TOK, head_count, HEAD_DIM).astype(jnp.float32)
        value_rows = window[:, :, 2].reshape(4 * FRAME_TOK, head_count, HEAD_DIM).astype(jnp.float32)
        scores = jnp.einsum("qhd,khd->hqk", queries, key_rows) * score_scale
        valid = (frame_index - 3 + key_frame) >= 0
        scores = jnp.where(valid[None, None, :], scores, -1e30)
        row_max = jnp.max(scores, axis=-1, keepdims=True)
        weights = jnp.exp(scores - row_max)
        row_sum = jnp.sum(weights, axis=-1, keepdims=True)
        probability = (weights / row_sum).astype(jnp.bfloat16)
        attended = jnp.einsum("hqk,khd->qhd", probability.astype(jnp.float32), value_rows).astype(jnp.bfloat16)
        attended = attended.reshape(FRAME_TOK, head_count * HEAD_DIM)
        branch = jnp.dot(attended, out_weight, preferred_element_type=jnp.float32)
        gate_row = lax.dynamic_index_in_dim(gate_table, timesteps[frame_index], 0, keepdims=True)
        frame_latents = lax.dynamic_index_in_dim(residual, frame_index, 0, keepdims=False)
        return (frame_latents.astype(jnp.float32) + gate_row * branch).astype(jnp.bfloat16)

    stacked = lax.map(one_frame, jnp.arange(frame_count, dtype=jnp.int32))
    return stacked.reshape(frame_count * FRAME_TOK, latents.shape[1])
```

```python
import functools
import math

import jax
import jax.numpy as jnp
from jax import lax
from jax.experimental import pallas as pl
from jax.experimental.pallas import tpu as pltpu
from jax.sharding import PartitionSpec as P

FRAME_TOK = 256


def passed_along(value, axis, steps):
    count = lax.axis_size(axis)
    initial, last = (max(0, -steps), min(count, count - steps))
    return lax.ppermute(value, axis, [(source, source + steps) for source in range(initial, last)])


def attend(queries, extended, first_frame, frame_count):
    pair_rows = 2 * FRAME_TOK
    key_count = 5 * FRAME_TOK
    score_scale = queries.shape[1] ** (-0.5)
    row_frame = jnp.arange(pair_rows, dtype=jnp.int32) // FRAME_TOK
    col_frame = jnp.arange(key_count, dtype=jnp.int32) // FRAME_TOK

    def frame_pair(pair_index):
        offset = pair_index * pair_rows
        query_block = lax.dynamic_slice_in_dim(queries, offset, pair_rows, 0)
        window = lax.dynamic_slice_in_dim(extended, offset, key_count, 0)
        key_block = window[:, 0]
        value_block = window[:, 1]
        scores = (
            lax.dot_general(
                query_block, key_block, (((1,), (1,)), ((), ())), preferred_element_type=jnp.float32
            )
            * score_scale
        )
        distance = col_frame[None, :] - row_frame[:, None]
        existing = first_frame + 2 * pair_index + col_frame - 3 >= 0
        allowed = (distance >= 0) & (distance <= 3) & existing[None, :]
        scores = jnp.where(allowed, scores, -1e30)
        row_max = jnp.max(scores, axis=-1, keepdims=True)
        weights = jnp.exp(scores - row_max)
        row_sum = jnp.sum(weights, axis=-1, keepdims=True)
        probability = (weights / row_sum).astype(jnp.bfloat16)
        return jnp.dot(probability, value_block, preferred_element_type=jnp.float32).astype(
            jnp.bfloat16
        )

    blocks = lax.map(frame_pair, jnp.arange(frame_count // 2, dtype=jnp.int32))
    return blocks.reshape(frame_count * FRAME_TOK, queries.shape[1])


def body(latents, projected, out_weight, gate_table, timesteps):
    row_count = latents.shape[0]
    frame_count = timesteps.shape[0]
    group_tokens = frame_count * FRAME_TOK
    head_view = lax.all_to_all(projected, "fsdp", split_axis=2, concat_axis=0, tiled=True)
    queries = head_view[:, 0]
    key_values = head_view[:, 1:3]
    trailing = passed_along(key_values[group_tokens - 3 * FRAME_TOK :], "tm", 1)
    extended = jnp.concatenate([trailing, key_values], axis=0)
    first_frame = lax.axis_index("tm") * frame_count
    attended = attend(queries, extended, first_frame, frame_count)
    gathered_heads = lax.all_to_all(attended, "fsdp", split_axis=0, concat_axis=1, tiled=True)
    update = jnp.dot(
        gathered_heads,
        lax.all_gather(out_weight, "fsdp", axis=1, tiled=True),
        preferred_element_type=jnp.float32,
    )
    step_count = gate_table.shape[0]
    step_onehot = (timesteps[:, None] == jnp.arange(step_count, dtype=jnp.int32)[None, :]).astype(
        jnp.float32
    )
    frame_gates = jnp.dot(step_onehot, gate_table, precision=lax.Precision.HIGHEST)
    row_frame = (
        lax.axis_index("fsdp") * row_count + jnp.arange(row_count, dtype=jnp.int32)
    ) // FRAME_TOK
    row_onehot = (row_frame[:, None] == jnp.arange(frame_count, dtype=jnp.int32)[None, :]).astype(
        jnp.float32
    )
    row_gates = jnp.dot(row_onehot, frame_gates, precision=lax.Precision.HIGHEST)
    return (latents.astype(jnp.float32) + row_gates * update).astype(jnp.bfloat16)


HEAD = 128
EARLY_WEIGHTS = (1, 2, 3)


def by_member(member, values):
    row, core = member // 2, member % 2
    v0, v1, v2, v3 = values
    return v0 + (v1 - v0) * core + (v2 - v0) * row + (v3 - v2 - v1 + v0) * core * row


def frame_kernel(
    groups,
    steps_ref,
    latents_hbm,
    qkv_hbm,
    weight_hbm,
    gates_hbm,
    out_hbm,
    qkv,
    kv,
    weight,
    latents,
    gates,
    gate_row,
    out,
    top,
    total,
    acc,
    attended,
    local_sem,
    out_sem,
    kv_send,
    kv_pass,
    kv_recv,
    w_send,
    w_pass,
    w_recv,
):
    heads = kv.shape[1]
    columns = weight.shape[2]
    half = columns // 2
    piece = half // 3
    group, member = lax.axis_index("tm"), lax.axis_index("fsdp")
    row, core = member // 2, member % 2
    across = group + 1 - 2 * (group % 2)
    sibling = member + 1 - 2 * core
    opposite = member + 2 - 4 * row
    far = 3 - member
    has_next = jnp.logical_and(member >= 1, group < groups - 1)
    has_previous = jnp.logical_and(member <= 2, group >= 1)

    def remote(source, target, send_sem, recv_sem, to_group, to_member):
        return pltpu.make_async_remote_copy(
            src_ref=source,
            dst_ref=target,
            send_sem=send_sem,
            recv_sem=recv_sem,
            device_id=(to_group, to_member),
            device_id_type=pl.DeviceIdType.MESH,
        )

    barrier = pltpu.get_barrier_semaphore()

    def greet(to_group, to_member):
        pl.semaphore_signal(
            barrier, inc=1, device_id=(to_group, to_member), device_id_type=pl.DeviceIdType.MESH
        )

    greet(group, sibling)
    greet(group, opposite)
    greet(across, member)

    @pl.when(has_next)
    def _():
        greet(group + 1, member - 1)

    @pl.when(has_previous)
    def _():
        greet(group - 1, member + 1)

    load_qkv = pltpu.make_async_copy(qkv_hbm, qkv, local_sem.at[0])
    load_weight = pltpu.make_async_copy(weight_hbm, weight.at[member], local_sem.at[1])
    load_latents = pltpu.make_async_copy(latents_hbm, latents, local_sem.at[2])
    load_gates = pltpu.make_async_copy(gates_hbm, gates, local_sem.at[3])
    load_qkv.start()
    load_weight.start()
    load_gates.start()
    load_latents.start()

    pl.semaphore_wait(barrier, 3 + has_next.astype(jnp.int32) + has_previous.astype(jnp.int32))

    sent = []

    def begin(condition, copy):
        sent.append((condition, copy))
        if condition is None:
            copy.start()
        else:
            pl.when(condition)(copy.start)

    for h in range(heads):
        own = qkv_hbm.at[pl.ds(1, 2), :, pl.ds(h * HEAD, HEAD)]
        begin(
            row == 0,
            remote(own, kv.at[1, h], kv_send.at[0, h], kv_recv.at[1, h], group, opposite),
        )
        begin(
            has_next,
            remote(own, kv.at[2, h], kv_send.at[1, h], kv_recv.at[2, h], group + 1, member - 1),
        )
        begin(
            core == 0,
            remote(own, kv.at[0, h], kv_send.at[2, h], kv_recv.at[0, h], group, sibling),
        )

    first = pl.multiple_of(half * (group % 2), 128)
    second = pl.multiple_of(half - half * (group % 2), 128)

    def cut(start, index):
        return pl.ds(pl.multiple_of(start + index * piece, 128), piece)

    for i in range(3):
        begin(
            None,
            remote(
                weight_hbm.at[:, cut(first, i)],
                weight.at[member, :, cut(first, i)],
                w_send.at[i],
                w_recv.at[i],
                group,
                opposite,
            ),
        )
    begin(
        None,
        remote(weight_hbm, weight.at[member], w_send.at[3], w_recv.at[6], group, sibling),
    )

    def arrived(target, sem):
        remote(target, target, w_send.at[0], sem, group, sibling).wait_recv()

    def take_piece(i):
        start = first if i < 3 else second
        block = weight.at[opposite, :, cut(start, i % 3)]
        arrived(block, w_recv.at[i])
        if i < 3:
            begin(
                None,
                remote(block, block, w_pass.at[i], w_recv.at[3 + i], across, member),
            )
        begin(
            None,
            remote(block, block, w_pass.at[3 + i], w_recv.at[7 + i], group, sibling),
        )

    scale = (HEAD ** -0.5) * math.log2(math.e)

    def own_head(index, h):
        return qkv[index, :, h * HEAD : (h + 1) * HEAD]

    def scores_of(h, keys):
        return (
            lax.dot_general(
                own_head(0, h), keys, (((1,), (1,)), ((), ())), preferred_element_type=jnp.float32
            )
            * scale
        )

    def start_head(h):
        scores = scores_of(h, own_head(1, h))
        row_top = jnp.max(scores, axis=-1, keepdims=True)
        weights = jnp.exp2(scores - row_top)
        top[h] = row_top
        total[h] = jnp.sum(weights, axis=-1, keepdims=True)
        acc[h] = jnp.dot(
            weights.astype(jnp.bfloat16), own_head(2, h), preferred_element_type=jnp.float32
        )

    def add_frame(h, slot):
        scores = scores_of(h, kv[slot, h, 0])
        old_top = top[h]
        row_top = jnp.maximum(old_top, jnp.max(scores, axis=-1, keepdims=True))
        weights = jnp.exp2(scores - row_top)
        shrink = jnp.exp2(old_top - row_top)
        top[h] = row_top
        total[h] = total[h] * shrink + jnp.sum(weights, axis=-1, keepdims=True)
        acc[h] = acc[h] * shrink + jnp.dot(
            weights.astype(jnp.bfloat16), kv[slot, h, 1], preferred_element_type=jnp.float32
        )

    order = ((3, 1, 2, 1), (1, 3, 3, 2), (2, 2, 1, 3))

    def take_frame(j, h):
        back = by_member(member, order[j])
        slot = back - 1
        exists = jnp.logical_or(group >= 1, member >= back)
        block = kv.at[slot, h]

        pl.when(exists)(lambda: arrived(block, kv_recv.at[slot, h]))
        if j == 0:
            begin(
                jnp.logical_and(exists, member == 2),
                remote(block, kv.at[2, h], kv_pass.at[0, h], kv_recv.at[2, h], group, sibling),
            )
        if j == 1:
            to = by_member(member, (1, 0, 0, 2))
            into = by_member(member, (1, 1, 0, 0))
            begin(
                exists,
                remote(block, kv.at[into, h], kv_pass.at[1, h], kv_recv.at[into, h], group, to),
            )
        pl.when(exists)(lambda: add_frame(h, slot))

    load_qkv.wait()
    for h in range(heads):
        start_head(h)
    load_gates.wait()
    step_index = lax.broadcasted_iota(jnp.int32, gates.shape, 0)
    gate_row[...] = jnp.sum(
        jnp.where(step_index == steps_ref[member], gates[...], 0.0), axis=0, keepdims=True
    )

    def finish_head(h):
        attended[:, h * HEAD : (h + 1) * HEAD] = (acc[h] / total[h]).astype(jnp.bfloat16)

    for h in range(heads):
        take_frame(0, h)
        take_frame(1, h)
        if h >= 1:
            take_frame(2, h - 1)
            finish_head(h - 1)
        if h in EARLY_WEIGHTS:
            take_piece(EARLY_WEIGHTS.index(h))
    take_frame(2, heads - 1)
    finish_head(heads - 1)

    writes = []

    def project(owner, start, width):
        place = pl.ds(pl.multiple_of(owner * columns + start, 128), width)
        branch = jnp.dot(
            attended[...],
            weight[owner, :, pl.ds(start, width)],
            preferred_element_type=jnp.float32,
        )
        out[:, place] = (
            latents[:, place].astype(jnp.float32) + gate_row[:, place] * branch
        ).astype(jnp.bfloat16)
        write = pltpu.make_async_copy(
            out.at[:, place], out_hbm.at[:, place], out_sem.at[len(writes)]
        )
        write.start()
        writes.append(write)

    load_weight.wait()
    load_latents.wait()
    project(member, 0, half)
    project(member, half, half)
    take_piece(3)
    arrived(weight.at[sibling], w_recv.at[6])
    project(sibling, 0, half)
    project(sibling, half, half)
    take_piece(4)
    project(opposite, first, half)
    take_piece(5)
    project(opposite, second, half)
    for i in range(3):
        arrived(weight.at[far, :, cut(first, i)], w_recv.at[7 + i])
    project(far, first, half)
    for i in range(3):
        arrived(weight.at[far, :, cut(second, i)], w_recv.at[10 + i])
    project(far, second, half)

    for condition, copy in sent:
        if condition is None:
            copy.wait_send()
        else:
            pl.when(condition)(copy.wait_send)
    for write in writes:
        write.wait()


def frame_body(latents, projected, out_weight, gate_table, timesteps, groups):
    rows, width = latents.shape
    inner, columns = out_weight.shape
    heads = inner // HEAD
    qkv = projected.transpose(1, 0, 2)
    anywhere = pl.BlockSpec(memory_space=pl.ANY)
    return pl.pallas_call(
        functools.partial(frame_kernel, groups),
        out_shape=jax.ShapeDtypeStruct((rows, width), jnp.bfloat16),
        in_specs=[pl.BlockSpec(memory_space=pltpu.SMEM)] + [anywhere] * 4,
        out_specs=anywhere,
        scratch_shapes=[
            pltpu.VMEM((3, rows, inner), jnp.bfloat16),
            pltpu.VMEM((3, heads, 2, rows, HEAD), jnp.bfloat16),
            pltpu.VMEM((4, inner, columns), jnp.bfloat16),
            pltpu.VMEM((rows, width), jnp.bfloat16),
            pltpu.VMEM(gate_table.shape, jnp.float32),
            pltpu.VMEM((1, width), jnp.float32),
            pltpu.VMEM((rows, width), jnp.bfloat16),
            pltpu.VMEM((heads, rows, 1), jnp.float32),
            pltpu.VMEM((heads, rows, 1), jnp.float32),
            pltpu.VMEM((heads, rows, HEAD), jnp.float32),
            pltpu.VMEM((rows, inner), jnp.bfloat16),
            pltpu.SemaphoreType.DMA((4,)),
            pltpu.SemaphoreType.DMA((8,)),
            pltpu.SemaphoreType.DMA((3, heads)),
            pltpu.SemaphoreType.DMA((2, heads)),
            pltpu.SemaphoreType.DMA((3, heads)),
            pltpu.SemaphoreType.DMA((4,)),
            pltpu.SemaphoreType.DMA((9,)),
            pltpu.SemaphoreType.DMA((13,)),
        ],
        compiler_params=pltpu.CompilerParams(
            collective_id=0, has_side_effects=True, vmem_limit_bytes=60 * 1024 * 1024
        ),
        cost_estimate=pl.CostEstimate(
            flops=2 * rows * inner * (8 * rows + width),
            bytes_accessed=4 * rows * width + 2 * inner * width,
            transcendentals=4 * heads * rows * rows,
        ),
    )(timesteps, latents, qkv, out_weight, gate_table)


def solution(mesh):
    in_specs = (
        P(("tm", "fsdp"), None),
        P(("tm", "fsdp"), None, None),
        P(None, "fsdp"),
        P(),
        P("tm"),
    )
    out_specs = P(("tm", "fsdp"), None)
    groups, members = mesh.shape["tm"], mesh.shape["fsdp"]

    def local(latents, projected, out_weight, gate_table, timesteps):
        one_frame_each = latents.shape[0] == FRAME_TOK and timesteps.shape[0] == members
        if one_frame_each and members == 4 and groups % 2 == 0:
            return frame_body(latents, projected, out_weight, gate_table, timesteps, groups)
        return body(latents, projected, out_weight, gate_table, timesteps)

    return jax.shard_map(local, mesh=mesh, in_specs=in_specs, out_specs=out_specs, check_vma=False)
```

```python
import functools
import math

import jax
import jax.numpy as jnp
from jax import lax
from jax.experimental import pallas as pl
from jax.experimental.pallas import tpu as pltpu
from jax.sharding import PartitionSpec as P

FRAME_TOK = 256


def passed_along(value, axis, steps):
    count = lax.axis_size(axis)
    initial, last = (max(0, -steps), min(count, count - steps))
    return lax.ppermute(value, axis, [(source, source + steps) for source in range(initial, last)])


def attend(queries, extended, first_frame, frame_count):
    pair_rows = 2 * FRAME_TOK
    key_count = 5 * FRAME_TOK
    score_scale = queries.shape[1] ** (-0.5)
    row_frame = jnp.arange(pair_rows, dtype=jnp.int32) // FRAME_TOK
    col_frame = jnp.arange(key_count, dtype=jnp.int32) // FRAME_TOK

    def frame_pair(pair_index):
        offset = pair_index * pair_rows
        query_block = lax.dynamic_slice_in_dim(queries, offset, pair_rows, 0)
        window = lax.dynamic_slice_in_dim(extended, offset, key_count, 0)
        key_block = window[:, 0]
        value_block = window[:, 1]
        scores = (
            lax.dot_general(
                query_block, key_block, (((1,), (1,)), ((), ())), preferred_element_type=jnp.float32
            )
            * score_scale
        )
        distance = col_frame[None, :] - row_frame[:, None]
        existing = first_frame + 2 * pair_index + col_frame - 3 >= 0
        allowed = (distance >= 0) & (distance <= 3) & existing[None, :]
        scores = jnp.where(allowed, scores, -1e30)
        row_max = jnp.max(scores, axis=-1, keepdims=True)
        weights = jnp.exp(scores - row_max)
        row_sum = jnp.sum(weights, axis=-1, keepdims=True)
        probability = (weights / row_sum).astype(jnp.bfloat16)
        return jnp.dot(probability, value_block, preferred_element_type=jnp.float32).astype(
            jnp.bfloat16
        )

    blocks = lax.map(frame_pair, jnp.arange(frame_count // 2, dtype=jnp.int32))
    return blocks.reshape(frame_count * FRAME_TOK, queries.shape[1])


def body(latents, projected, out_weight, gate_table, timesteps):
    row_count = latents.shape[0]
    frame_count = timesteps.shape[0]
    group_tokens = frame_count * FRAME_TOK
    head_view = lax.all_to_all(projected, "fsdp", split_axis=2, concat_axis=0, tiled=True)
    queries = head_view[:, 0]
    key_values = head_view[:, 1:3]
    trailing = passed_along(key_values[group_tokens - 3 * FRAME_TOK :], "tm", 1)
    extended = jnp.concatenate([trailing, key_values], axis=0)
    first_frame = lax.axis_index("tm") * frame_count
    attended = attend(queries, extended, first_frame, frame_count)
    gathered_heads = lax.all_to_all(attended, "fsdp", split_axis=0, concat_axis=1, tiled=True)
    update = jnp.dot(
        gathered_heads,
        lax.all_gather(out_weight, "fsdp", axis=1, tiled=True),
        preferred_element_type=jnp.float32,
    )
    step_count = gate_table.shape[0]
    step_onehot = (timesteps[:, None] == jnp.arange(step_count, dtype=jnp.int32)[None, :]).astype(
        jnp.float32
    )
    frame_gates = jnp.dot(step_onehot, gate_table, precision=lax.Precision.HIGHEST)
    row_frame = (
        lax.axis_index("fsdp") * row_count + jnp.arange(row_count, dtype=jnp.int32)
    ) // FRAME_TOK
    row_onehot = (row_frame[:, None] == jnp.arange(frame_count, dtype=jnp.int32)[None, :]).astype(
        jnp.float32
    )
    row_gates = jnp.dot(row_onehot, frame_gates, precision=lax.Precision.HIGHEST)
    return (latents.astype(jnp.float32) + row_gates * update).astype(jnp.bfloat16)


HEAD = 128


def by_member(member, values):
    row, core = member // 2, member % 2
    v0, v1, v2, v3 = values
    return v0 + (v1 - v0) * core + (v2 - v0) * row + (v3 - v2 - v1 + v0) * core * row


def frame_kernel(
    groups,
    steps_ref,
    latents_hbm,
    qkv_hbm,
    weight_hbm,
    gates_hbm,
    out,
    qkv,
    kv,
    weight,
    latents,
    gates,
    gate_row,
    top,
    total,
    acc,
    attended,
    local_sem,
    kv_send,
    kv_pass,
    kv_recv,
    w_send,
    w_pass,
    w_recv,
):
    heads = kv.shape[1]
    columns = weight.shape[2]
    half = columns // 2
    piece = half // 3
    group, member = lax.axis_index("tm"), lax.axis_index("fsdp")
    row, core = member // 2, member % 2
    across = group + 1 - 2 * (group % 2)
    sibling = member + 1 - 2 * core
    opposite = member + 2 - 4 * row
    far = 3 - member
    has_next = jnp.logical_and(member >= 1, group < groups - 1)
    has_previous = jnp.logical_and(member <= 2, group >= 1)

    def remote(source, target, send_sem, recv_sem, to_group, to_member):
        return pltpu.make_async_remote_copy(
            src_ref=source,
            dst_ref=target,
            send_sem=send_sem,
            recv_sem=recv_sem,
            device_id=(to_group, to_member),
            device_id_type=pl.DeviceIdType.MESH,
        )

    barrier = pltpu.get_barrier_semaphore()

    def greet(to_group, to_member):
        pl.semaphore_signal(
            barrier, inc=1, device_id=(to_group, to_member), device_id_type=pl.DeviceIdType.MESH
        )

    greet(group, sibling)
    greet(group, opposite)
    greet(across, member)

    @pl.when(has_next)
    def _():
        greet(group + 1, member - 1)

    @pl.when(has_previous)
    def _():
        greet(group - 1, member + 1)

    load_qkv = pltpu.make_async_copy(qkv_hbm, qkv, local_sem.at[0])
    load_weight = pltpu.make_async_copy(weight_hbm, weight.at[member], local_sem.at[1])
    load_latents = pltpu.make_async_copy(latents_hbm, latents, local_sem.at[2])
    load_gates = pltpu.make_async_copy(gates_hbm, gates, local_sem.at[3])
    load_qkv.start()
    load_weight.start()
    load_gates.start()
    load_latents.start()

    pl.semaphore_wait(barrier, 3 + has_next.astype(jnp.int32) + has_previous.astype(jnp.int32))

    sent = []

    def begin(condition, copy):
        sent.append((condition, copy))
        if condition is None:
            copy.start()
        else:
            pl.when(condition)(copy.start)

    for h in range(heads):
        own = qkv_hbm.at[pl.ds(1, 2), :, pl.ds(h * HEAD, HEAD)]
        begin(
            row == 0,
            remote(own, kv.at[1, h], kv_send.at[0, h], kv_recv.at[1, h], group, opposite),
        )
        begin(
            has_next,
            remote(own, kv.at[2, h], kv_send.at[1, h], kv_recv.at[2, h], group + 1, member - 1),
        )
        begin(
            core == 0,
            remote(own, kv.at[0, h], kv_send.at[2, h], kv_recv.at[0, h], group, sibling),
        )

    first = pl.multiple_of(half * (group % 2), 128)
    second = pl.multiple_of(half - half * (group % 2), 128)

    def cut(start, index):
        return pl.ds(pl.multiple_of(start + index * piece, 128), piece)

    def send_piece(i):
        begin(
            None,
            remote(
                weight_hbm.at[:, cut(first, i)],
                weight.at[member, :, cut(first, i)],
                w_send.at[i],
                w_recv.at[i],
                group,
                opposite,
            ),
        )

    def send_sibling():
        begin(
            None,
            remote(weight_hbm, weight.at[member], w_send.at[3], w_recv.at[6], group, sibling),
        )

    def arrived(target, sem):
        remote(target, target, w_send.at[0], sem, group, sibling).wait_recv()

    def take_piece(i):
        start = first if i < 3 else second
        block = weight.at[opposite, :, cut(start, i % 3)]
        arrived(block, w_recv.at[i])
        if i < 3:
            begin(
                None,
                remote(block, block, w_pass.at[i], w_recv.at[3 + i], across, member),
            )
        begin(
            None,
            remote(block, block, w_pass.at[3 + i], w_recv.at[7 + i], group, sibling),
        )

    scale = (HEAD ** -0.5) * math.log2(math.e)

    def own_head(index, h):
        return qkv[index, :, h * HEAD : (h + 1) * HEAD]

    def scores_of(h, keys):
        return (
            lax.dot_general(
                own_head(0, h), keys, (((1,), (1,)), ((), ())), preferred_element_type=jnp.float32
            )
            * scale
        )

    def start_head(h):
        scores = scores_of(h, own_head(1, h))
        row_top = jnp.max(scores, axis=-1, keepdims=True)
        weights = jnp.exp2(scores - row_top)
        top[h] = row_top
        total[h] = jnp.sum(weights, axis=-1, keepdims=True)
        acc[h] = jnp.dot(
            weights.astype(jnp.bfloat16), own_head(2, h), preferred_element_type=jnp.float32
        )

    def add_frame(h, slot):
        scores = scores_of(h, kv[slot, h, 0])
        old_top = top[h]
        row_top = jnp.maximum(old_top, jnp.max(scores, axis=-1, keepdims=True))
        weights = jnp.exp2(scores - row_top)
        shrink = jnp.exp2(old_top - row_top)
        top[h] = row_top
        total[h] = total[h] * shrink + jnp.sum(weights, axis=-1, keepdims=True)
        acc[h] = acc[h] * shrink + jnp.dot(
            weights.astype(jnp.bfloat16), kv[slot, h, 1], preferred_element_type=jnp.float32
        )

    order = ((3, 1, 2, 1), (1, 3, 3, 2), (2, 2, 1, 3))

    def place_of(j):
        back = by_member(member, order[j])
        return back - 1, jnp.logical_or(group >= 1, member >= back)

    def receive(j, h):
        slot, exists = place_of(j)
        block = kv.at[slot, h]
        pl.when(exists)(lambda: arrived(block, kv_recv.at[slot, h]))
        if j == 0:
            begin(
                jnp.logical_and(exists, member == 2),
                remote(block, kv.at[2, h], kv_pass.at[0, h], kv_recv.at[2, h], group, sibling),
            )
        if j == 1:
            to = by_member(member, (1, 0, 0, 2))
            into = by_member(member, (1, 1, 0, 0))
            begin(
                exists,
                remote(block, kv.at[into, h], kv_pass.at[1, h], kv_recv.at[into, h], group, to),
            )

    def attend_frame(j, h):
        slot, exists = place_of(j)
        pl.when(exists)(lambda: add_frame(h, slot))

    load_qkv.wait()
    for h in range(heads):
        start_head(h)
    load_gates.wait()
    step_index = lax.broadcasted_iota(jnp.int32, gates.shape, 0)
    gate_row[...] = jnp.sum(
        jnp.where(step_index == steps_ref[member], gates[...], 0.0), axis=0, keepdims=True
    )

    def finish_head(h):
        attended[:, h * HEAD : (h + 1) * HEAD] = (acc[h] / total[h]).astype(jnp.bfloat16)

    for h in range(heads):
        receive(0, h)
        receive(1, h)
        if h == 1:
            send_sibling()
        if h >= 1:
            send_piece(h - 1)
            receive(2, h - 1)
        attend_frame(0, h)
        attend_frame(1, h)
        if h >= 1:
            attend_frame(2, h - 1)
            finish_head(h - 1)
    receive(2, heads - 1)
    attend_frame(2, heads - 1)
    finish_head(heads - 1)

    def project(owner, start, width):
        place = pl.ds(pl.multiple_of(owner * columns + start, 128), width)
        branch = jnp.dot(
            attended[...],
            weight[owner, :, pl.ds(start, width)],
            preferred_element_type=jnp.float32,
        )
        out[:, place] = (
            latents[:, place].astype(jnp.float32) + gate_row[:, place] * branch
        ).astype(jnp.bfloat16)

    load_weight.wait()
    load_latents.wait()
    take_piece(0)
    project(member, 0, half)
    take_piece(1)
    project(member, half, half)
    take_piece(2)
    arrived(weight.at[sibling], w_recv.at[6])
    project(sibling, 0, half)
    project(sibling, half, half)
    take_piece(3)
    project(opposite, first, half)
    take_piece(4)
    for i in range(3):
        arrived(weight.at[far, :, cut(first, i)], w_recv.at[7 + i])
    project(far, first, half)
    take_piece(5)
    project(opposite, second, half)
    for i in range(3):
        arrived(weight.at[far, :, cut(second, i)], w_recv.at[10 + i])
    project(far, second, half)

    for condition, copy in sent:
        if condition is None:
            copy.wait_send()
        else:
            pl.when(condition)(copy.wait_send)


def frame_body(latents, projected, out_weight, gate_table, timesteps, groups):
    rows, width = latents.shape
    inner, columns = out_weight.shape
    heads = inner // HEAD
    qkv = projected.transpose(1, 0, 2)
    in_hbm = pl.BlockSpec(memory_space=pltpu.HBM)
    return pl.pallas_call(
        functools.partial(frame_kernel, groups),
        out_shape=pltpu.VMEM((rows, width), jnp.bfloat16),
        in_specs=[pl.BlockSpec(memory_space=pltpu.SMEM)] + [in_hbm] * 4,
        out_specs=pl.BlockSpec(memory_space=pltpu.VMEM),
        scratch_shapes=[
            pltpu.VMEM((3, rows, inner), jnp.bfloat16),
            pltpu.VMEM((3, heads, 2, rows, HEAD), jnp.bfloat16),
            pltpu.VMEM((4, inner, columns), jnp.bfloat16),
            pltpu.VMEM((rows, width), jnp.bfloat16),
            pltpu.VMEM(gate_table.shape, jnp.float32),
            pltpu.VMEM((1, width), jnp.float32),
            pltpu.VMEM((heads, rows, 1), jnp.float32),
            pltpu.VMEM((heads, rows, 1), jnp.float32),
            pltpu.VMEM((heads, rows, HEAD), jnp.float32),
            pltpu.VMEM((rows, inner), jnp.bfloat16),
            pltpu.SemaphoreType.DMA((4,)),
            pltpu.SemaphoreType.DMA((3, heads)),
            pltpu.SemaphoreType.DMA((2, heads)),
            pltpu.SemaphoreType.DMA((3, heads)),
            pltpu.SemaphoreType.DMA((4,)),
            pltpu.SemaphoreType.DMA((9,)),
            pltpu.SemaphoreType.DMA((13,)),
        ],
        compiler_params=pltpu.CompilerParams(
            collective_id=0, has_side_effects=True, vmem_limit_bytes=56 * 1024 * 1024
        ),
        cost_estimate=pl.CostEstimate(
            flops=2 * rows * inner * (8 * rows + width),
            bytes_accessed=4 * rows * width + 2 * inner * width,
            transcendentals=4 * heads * rows * rows,
        ),
    )(timesteps, latents, qkv, out_weight, gate_table)


def solution(mesh):
    in_specs = (
        P(("tm", "fsdp"), None),
        P(("tm", "fsdp"), None, None),
        P(None, "fsdp"),
        P(),
        P("tm"),
    )
    out_specs = P(("tm", "fsdp"), None)
    groups, members = mesh.shape["tm"], mesh.shape["fsdp"]

    def local(latents, projected, out_weight, gate_table, timesteps):
        one_frame_each = latents.shape[0] == FRAME_TOK and timesteps.shape[0] == members
        if one_frame_each and members == 4 and groups % 2 == 0:
            return frame_body(latents, projected, out_weight, gate_table, timesteps, groups)
        return body(latents, projected, out_weight, gate_table, timesteps)

    return jax.shard_map(local, mesh=mesh, in_specs=in_specs, out_specs=out_specs, check_vma=False)
```

```python
import functools
import math

import jax
import jax.numpy as jnp
from jax import lax
from jax.experimental import pallas as pl
from jax.experimental.pallas import tpu as pltpu
from jax.sharding import PartitionSpec as P

FRAME_TOK = 256


def passed_along(value, axis, steps):
    count = lax.axis_size(axis)
    initial, last = (max(0, -steps), min(count, count - steps))
    return lax.ppermute(value, axis, [(source, source + steps) for source in range(initial, last)])


def attend(queries, extended, first_frame, frame_count):
    pair_rows = 2 * FRAME_TOK
    key_count = 5 * FRAME_TOK
    score_scale = queries.shape[1] ** (-0.5)
    row_frame = jnp.arange(pair_rows, dtype=jnp.int32) // FRAME_TOK
    col_frame = jnp.arange(key_count, dtype=jnp.int32) // FRAME_TOK

    def frame_pair(pair_index):
        offset = pair_index * pair_rows
        query_block = lax.dynamic_slice_in_dim(queries, offset, pair_rows, 0)
        window = lax.dynamic_slice_in_dim(extended, offset, key_count, 0)
        key_block = window[:, 0]
        value_block = window[:, 1]
        scores = (
            lax.dot_general(
                query_block, key_block, (((1,), (1,)), ((), ())), preferred_element_type=jnp.float32
            )
            * score_scale
        )
        distance = col_frame[None, :] - row_frame[:, None]
        existing = first_frame + 2 * pair_index + col_frame - 3 >= 0
        allowed = (distance >= 0) & (distance <= 3) & existing[None, :]
        scores = jnp.where(allowed, scores, -1e30)
        row_max = jnp.max(scores, axis=-1, keepdims=True)
        weights = jnp.exp(scores - row_max)
        row_sum = jnp.sum(weights, axis=-1, keepdims=True)
        probability = (weights / row_sum).astype(jnp.bfloat16)
        return jnp.dot(probability, value_block, preferred_element_type=jnp.float32).astype(
            jnp.bfloat16
        )

    blocks = lax.map(frame_pair, jnp.arange(frame_count // 2, dtype=jnp.int32))
    return blocks.reshape(frame_count * FRAME_TOK, queries.shape[1])


def body(latents, projected, out_weight, gate_table, timesteps):
    row_count = latents.shape[0]
    frame_count = timesteps.shape[0]
    group_tokens = frame_count * FRAME_TOK
    head_view = lax.all_to_all(projected, "fsdp", split_axis=2, concat_axis=0, tiled=True)
    queries = head_view[:, 0]
    key_values = head_view[:, 1:3]
    trailing = passed_along(key_values[group_tokens - 3 * FRAME_TOK :], "tm", 1)
    extended = jnp.concatenate([trailing, key_values], axis=0)
    first_frame = lax.axis_index("tm") * frame_count
    attended = attend(queries, extended, first_frame, frame_count)
    gathered_heads = lax.all_to_all(attended, "fsdp", split_axis=0, concat_axis=1, tiled=True)
    update = jnp.dot(
        gathered_heads,
        lax.all_gather(out_weight, "fsdp", axis=1, tiled=True),
        preferred_element_type=jnp.float32,
    )
    step_count = gate_table.shape[0]
    step_onehot = (timesteps[:, None] == jnp.arange(step_count, dtype=jnp.int32)[None, :]).astype(
        jnp.float32
    )
    frame_gates = jnp.dot(step_onehot, gate_table, precision=lax.Precision.HIGHEST)
    row_frame = (
        lax.axis_index("fsdp") * row_count + jnp.arange(row_count, dtype=jnp.int32)
    ) // FRAME_TOK
    row_onehot = (row_frame[:, None] == jnp.arange(frame_count, dtype=jnp.int32)[None, :]).astype(
        jnp.float32
    )
    row_gates = jnp.dot(row_onehot, frame_gates, precision=lax.Precision.HIGHEST)
    return (latents.astype(jnp.float32) + row_gates * update).astype(jnp.bfloat16)


HEAD = 128


def by_member(member, values):
    row, core = member // 2, member % 2
    v0, v1, v2, v3 = values
    return v0 + (v1 - v0) * core + (v2 - v0) * row + (v3 - v2 - v1 + v0) * core * row


def frame_kernel(
    groups,
    steps_ref,
    latents_hbm,
    qkv_hbm,
    weight_hbm,
    gates_hbm,
    out,
    qkv,
    kv,
    weight,
    latents,
    gates,
    gate_row,
    top,
    total,
    acc,
    attended,
    local_sem,
    kv_send,
    kv_pass,
    kv_recv,
    w_send,
    w_pass,
    w_recv,
):
    heads = kv.shape[1]
    columns = weight.shape[2]
    half = columns // 2
    piece = half // 3
    group, member = lax.axis_index("tm"), lax.axis_index("fsdp")
    row, core = member // 2, member % 2
    across = group + 1 - 2 * (group % 2)
    sibling = member + 1 - 2 * core
    opposite = member + 2 - 4 * row
    far = 3 - member
    has_next = jnp.logical_and(member >= 1, group < groups - 1)
    has_previous = jnp.logical_and(member <= 2, group >= 1)

    def remote(source, target, send_sem, recv_sem, to_group, to_member):
        return pltpu.make_async_remote_copy(
            src_ref=source,
            dst_ref=target,
            send_sem=send_sem,
            recv_sem=recv_sem,
            device_id=(to_group, to_member),
            device_id_type=pl.DeviceIdType.MESH,
        )

    barrier = pltpu.get_barrier_semaphore()

    def greet(to_group, to_member):
        pl.semaphore_signal(
            barrier, inc=1, device_id=(to_group, to_member), device_id_type=pl.DeviceIdType.MESH
        )

    greet(group, sibling)
    greet(group, opposite)
    greet(across, member)

    @pl.when(has_next)
    def _():
        greet(group + 1, member - 1)

    @pl.when(has_previous)
    def _():
        greet(group - 1, member + 1)

    load_qkv = pltpu.make_async_copy(qkv_hbm, qkv, local_sem.at[0])
    load_weight = pltpu.make_async_copy(weight_hbm, weight.at[member], local_sem.at[1])
    load_latents = pltpu.make_async_copy(latents_hbm, latents, local_sem.at[2])
    load_gates = pltpu.make_async_copy(gates_hbm, gates, local_sem.at[3])
    load_qkv.start()
    load_weight.start()
    load_gates.start()
    load_latents.start()

    pl.semaphore_wait(barrier, 3 + has_next.astype(jnp.int32) + has_previous.astype(jnp.int32))

    sent = []

    def begin(condition, copy):
        sent.append((condition, copy))
        if condition is None:
            copy.start()
        else:
            pl.when(condition)(copy.start)

    def own_block(h):
        return qkv_hbm.at[pl.ds(1, 2), :, pl.ds(h * HEAD, HEAD)]

    def send_opposite(h):
        begin(
            row == 0,
            remote(own_block(h), kv.at[1, h], kv_send.at[0, h], kv_recv.at[1, h], group, opposite),
        )

    def send_near(h):
        begin(
            has_next,
            remote(
                own_block(h), kv.at[2, h], kv_send.at[1, h], kv_recv.at[2, h], group + 1, member - 1
            ),
        )
        begin(
            core == 0,
            remote(own_block(h), kv.at[0, h], kv_send.at[2, h], kv_recv.at[0, h], group, sibling),
        )

    first = pl.multiple_of(half * (group % 2), 128)
    second = pl.multiple_of(half - half * (group % 2), 128)

    def cut(start, index):
        return pl.ds(pl.multiple_of(start + index * piece, 128), piece)

    def send_piece(i):
        begin(
            None,
            remote(
                weight_hbm.at[:, cut(first, i)],
                weight.at[member, :, cut(first, i)],
                w_send.at[i],
                w_recv.at[i],
                group,
                opposite,
            ),
        )

    def send_sibling():
        begin(
            None,
            remote(weight_hbm, weight.at[member], w_send.at[3], w_recv.at[6], group, sibling),
        )

    def arrived(target, sem):
        remote(target, target, w_send.at[0], sem, group, sibling).wait_recv()

    def take_piece(i):
        start = first if i < 3 else second
        block = weight.at[opposite, :, cut(start, i % 3)]
        arrived(block, w_recv.at[i])
        if i < 3:
            begin(
                None,
                remote(block, block, w_pass.at[i], w_recv.at[3 + i], across, member),
            )
        begin(
            None,
            remote(block, block, w_pass.at[3 + i], w_recv.at[7 + i], group, sibling),
        )

    scale = (HEAD ** -0.5) * math.log2(math.e)

    def own_head(index, h):
        return qkv[index, :, h * HEAD : (h + 1) * HEAD]

    def scores_of(h, keys):
        return (
            lax.dot_general(
                keys, own_head(0, h), (((1,), (1,)), ((), ())), preferred_element_type=jnp.float32
            )
            * scale
        )

    def mix(values, weights):
        return lax.dot_general(
            values,
            weights.astype(jnp.bfloat16),
            (((0,), (0,)), ((), ())),
            preferred_element_type=jnp.float32,
        )

    def start_head(h):
        scores = scores_of(h, own_head(1, h))
        row_top = jnp.max(scores, axis=0, keepdims=True)
        weights = jnp.exp2(scores - row_top)
        top[h] = row_top
        total[h] = jnp.sum(weights, axis=0, keepdims=True)
        acc[h] = mix(own_head(2, h), weights)

    def add_frame(h, slot):
        scores = scores_of(h, kv[slot, h, 0])
        old_top = top[h]
        row_top = jnp.maximum(old_top, jnp.max(scores, axis=0, keepdims=True))
        weights = jnp.exp2(scores - row_top)
        shrink = jnp.exp2(old_top - row_top)
        top[h] = row_top
        total[h] = total[h] * shrink + jnp.sum(weights, axis=0, keepdims=True)
        acc[h] = acc[h] * shrink + mix(kv[slot, h, 1], weights)

    order = ((3, 1, 3, 1), (1, 3, 2, 2), (2, 2, 1, 3))

    def place_of(j):
        back = by_member(member, order[j])
        return back - 1, jnp.logical_or(group >= 1, member >= back)

    def receive(j, h):
        slot, exists = place_of(j)
        block = kv.at[slot, h]
        pl.when(exists)(lambda: arrived(block, kv_recv.at[slot, h]))
        if j == 0:
            begin(
                jnp.logical_and(exists, member == 2),
                remote(block, kv.at[0, h], kv_pass.at[0, h], kv_recv.at[0, h], group, opposite),
            )
        if j == 1:
            into = by_member(member, (1, 1, 2, 0))
            begin(
                exists,
                remote(
                    block, kv.at[into, h], kv_pass.at[1, h], kv_recv.at[into, h], group, sibling
                ),
            )

    def attend_frame(j, h):
        slot, exists = place_of(j)
        pl.when(exists)(lambda: add_frame(h, slot))

    def finish_head(h):
        attended[:, h * HEAD : (h + 1) * HEAD] = jnp.transpose(acc[h] / total[h]).astype(jnp.bfloat16)

    for i in range(3):
        send_piece(i)
        send_near(i)
    for h in range(3, heads):
        send_near(h)
    send_opposite(0)
    send_sibling()

    load_qkv.wait()
    start_head(0)
    start_head(1)
    receive(0, 0)
    receive(0, 1)
    take_piece(0)
    send_opposite(1)
    for h in range(2, heads):
        start_head(h)
        receive(0, h)
    attend_frame(0, 0)
    attend_frame(0, 1)
    take_piece(1)
    send_opposite(2)
    for h in range(2, heads):
        attend_frame(0, h)
    load_gates.wait()
    step_index = lax.broadcasted_iota(jnp.int32, gates.shape, 0)
    gate_row[...] = jnp.sum(
        jnp.where(step_index == steps_ref[member], gates[...], 0.0), axis=0, keepdims=True
    )
    take_piece(2)
    for h in range(3, heads):
        send_opposite(h)
    for h in range(heads):
        receive(1, h)
        if h >= 1:
            receive(2, h - 1)
            take_piece(2 + min(h, 3))
        attend_frame(1, h)
        if h >= 1:
            attend_frame(2, h - 1)
            finish_head(h - 1)
    receive(2, heads - 1)
    attend_frame(2, heads - 1)
    finish_head(heads - 1)

    def project(owner, start, width):
        place = pl.ds(pl.multiple_of(owner * columns + start, 128), width)
        branch = jnp.dot(
            attended[...],
            weight[owner, :, pl.ds(start, width)],
            preferred_element_type=jnp.float32,
        )
        out[:, place] = (
            latents[:, place].astype(jnp.float32) + gate_row[:, place] * branch
        ).astype(jnp.bfloat16)

    load_weight.wait()
    load_latents.wait()
    project(member, 0, half)
    project(member, half, half)
    arrived(weight.at[sibling], w_recv.at[6])
    project(sibling, 0, half)
    project(sibling, half, half)
    project(opposite, first, half)
    project(opposite, second, half)
    for i in range(6):
        arrived(weight.at[far, :, cut(first if i < 3 else second, i % 3)], w_recv.at[7 + i])
        if i % 3 == 2:
            project(far, first if i < 3 else second, half)

    for condition, copy in sent:
        if condition is None:
            copy.wait_send()
        else:
            pl.when(condition)(copy.wait_send)


def frame_body(latents, projected, out_weight, gate_table, timesteps, groups):
    rows, width = latents.shape
    inner, columns = out_weight.shape
    heads = inner // HEAD
    qkv = projected.transpose(1, 0, 2)
    in_hbm = pl.BlockSpec(memory_space=pltpu.HBM)
    return pl.pallas_call(
        functools.partial(frame_kernel, groups),
        out_shape=pltpu.VMEM((rows, width), jnp.bfloat16),
        in_specs=[pl.BlockSpec(memory_space=pltpu.SMEM)] + [in_hbm] * 4,
        out_specs=pl.BlockSpec(memory_space=pltpu.VMEM),
        scratch_shapes=[
            pltpu.VMEM((3, rows, inner), jnp.bfloat16),
            pltpu.VMEM((3, heads, 2, rows, HEAD), jnp.bfloat16),
            pltpu.VMEM((4, inner, columns), jnp.bfloat16),
            pltpu.VMEM((rows, width), jnp.bfloat16),
            pltpu.VMEM(gate_table.shape, jnp.float32),
            pltpu.VMEM((1, width), jnp.float32),
            pltpu.VMEM((heads, 1, rows), jnp.float32),
            pltpu.VMEM((heads, 1, rows), jnp.float32),
            pltpu.VMEM((heads, HEAD, rows), jnp.float32),
            pltpu.VMEM((rows, inner), jnp.bfloat16),
            pltpu.SemaphoreType.DMA((4,)),
            pltpu.SemaphoreType.DMA((3, heads)),
            pltpu.SemaphoreType.DMA((2, heads)),
            pltpu.SemaphoreType.DMA((3, heads)),
            pltpu.SemaphoreType.DMA((4,)),
            pltpu.SemaphoreType.DMA((9,)),
            pltpu.SemaphoreType.DMA((13,)),
        ],
        compiler_params=pltpu.CompilerParams(
            collective_id=0, has_side_effects=True, vmem_limit_bytes=56 * 1024 * 1024
        ),
        cost_estimate=pl.CostEstimate(
            flops=2 * rows * inner * (8 * rows + width),
            bytes_accessed=4 * rows * width + 2 * inner * width,
            transcendentals=4 * heads * rows * rows,
        ),
    )(timesteps, latents, qkv, out_weight, gate_table)


def solution(mesh):
    in_specs = (
        P(("tm", "fsdp"), None),
        P(("tm", "fsdp"), None, None),
        P(None, "fsdp"),
        P(),
        P("tm"),
    )
    out_specs = P(("tm", "fsdp"), None)
    groups, members = mesh.shape["tm"], mesh.shape["fsdp"]

    def local(latents, projected, out_weight, gate_table, timesteps):
        one_frame_each = latents.shape[0] == FRAME_TOK and timesteps.shape[0] == members
        if one_frame_each and members == 4 and groups % 2 == 0:
            return frame_body(latents, projected, out_weight, gate_table, timesteps, groups)
        return body(latents, projected, out_weight, gate_table, timesteps)

    return jax.shard_map(local, mesh=mesh, in_specs=in_specs, out_specs=out_specs, check_vma=False)
```

```python
import functools
import math

import jax
import jax.numpy as jnp
from jax import lax
from jax.experimental import pallas as pl
from jax.experimental.pallas import tpu as pltpu
from jax.sharding import PartitionSpec as P

FRAME_TOK = 256


def passed_along(value, axis, steps):
    count = lax.axis_size(axis)
    initial, last = (max(0, -steps), min(count, count - steps))
    return lax.ppermute(value, axis, [(source, source + steps) for source in range(initial, last)])


def attend(queries, extended, first_frame, frame_count):
    pair_rows = 2 * FRAME_TOK
    key_count = 5 * FRAME_TOK
    score_scale = queries.shape[1] ** (-0.5)
    row_frame = jnp.arange(pair_rows, dtype=jnp.int32) // FRAME_TOK
    col_frame = jnp.arange(key_count, dtype=jnp.int32) // FRAME_TOK

    def frame_pair(pair_index):
        offset = pair_index * pair_rows
        query_block = lax.dynamic_slice_in_dim(queries, offset, pair_rows, 0)
        window = lax.dynamic_slice_in_dim(extended, offset, key_count, 0)
        key_block = window[:, 0]
        value_block = window[:, 1]
        scores = (
            lax.dot_general(
                query_block, key_block, (((1,), (1,)), ((), ())), preferred_element_type=jnp.float32
            )
            * score_scale
        )
        distance = col_frame[None, :] - row_frame[:, None]
        existing = first_frame + 2 * pair_index + col_frame - 3 >= 0
        allowed = (distance >= 0) & (distance <= 3) & existing[None, :]
        scores = jnp.where(allowed, scores, -1e30)
        row_max = jnp.max(scores, axis=-1, keepdims=True)
        weights = jnp.exp(scores - row_max)
        row_sum = jnp.sum(weights, axis=-1, keepdims=True)
        probability = (weights / row_sum).astype(jnp.bfloat16)
        return jnp.dot(probability, value_block, preferred_element_type=jnp.float32).astype(
            jnp.bfloat16
        )

    blocks = lax.map(frame_pair, jnp.arange(frame_count // 2, dtype=jnp.int32))
    return blocks.reshape(frame_count * FRAME_TOK, queries.shape[1])


def body(latents, projected, out_weight, gate_table, timesteps):
    row_count = latents.shape[0]
    frame_count = timesteps.shape[0]
    group_tokens = frame_count * FRAME_TOK
    head_view = lax.all_to_all(projected, "fsdp", split_axis=2, concat_axis=0, tiled=True)
    queries = head_view[:, 0]
    key_values = head_view[:, 1:3]
    trailing = passed_along(key_values[group_tokens - 3 * FRAME_TOK :], "tm", 1)
    extended = jnp.concatenate([trailing, key_values], axis=0)
    first_frame = lax.axis_index("tm") * frame_count
    attended = attend(queries, extended, first_frame, frame_count)
    gathered_heads = lax.all_to_all(attended, "fsdp", split_axis=0, concat_axis=1, tiled=True)
    update = jnp.dot(
        gathered_heads,
        lax.all_gather(out_weight, "fsdp", axis=1, tiled=True),
        preferred_element_type=jnp.float32,
    )
    step_count = gate_table.shape[0]
    step_onehot = (timesteps[:, None] == jnp.arange(step_count, dtype=jnp.int32)[None, :]).astype(
        jnp.float32
    )
    frame_gates = jnp.dot(step_onehot, gate_table, precision=lax.Precision.HIGHEST)
    row_frame = (
        lax.axis_index("fsdp") * row_count + jnp.arange(row_count, dtype=jnp.int32)
    ) // FRAME_TOK
    row_onehot = (row_frame[:, None] == jnp.arange(frame_count, dtype=jnp.int32)[None, :]).astype(
        jnp.float32
    )
    row_gates = jnp.dot(row_onehot, frame_gates, precision=lax.Precision.HIGHEST)
    return (latents.astype(jnp.float32) + row_gates * update).astype(jnp.bfloat16)


HEAD = 128


def by_member(member, values):
    row, core = member // 2, member % 2
    v0, v1, v2, v3 = values
    return v0 + (v1 - v0) * core + (v2 - v0) * row + (v3 - v2 - v1 + v0) * core * row


def frame_kernel(
    groups,
    steps_ref,
    latents_hbm,
    qkv_hbm,
    weight_hbm,
    gates_hbm,
    out,
    qkv,
    kv,
    weight,
    latents,
    gates,
    gate_row,
    top,
    total,
    acc,
    attended,
    local_sem,
    kv_send,
    kv_pass,
    kv_recv,
    w_send,
    w_pass,
    w_recv,
):
    heads = kv.shape[1]
    columns = weight.shape[2]
    half = columns // 2
    piece = weight.shape[1] // 8
    group, member = lax.axis_index("tm"), lax.axis_index("fsdp")
    row, core = member // 2, member % 2
    beside = group + 1 - 2 * (group % 2)
    along = group + 2 - 4 * ((group // 2) % 2)
    sibling = member + 1 - 2 * core
    opposite = member + 2 - 4 * row
    far = 3 - member
    has_next = jnp.logical_and(member >= 1, group < groups - 1)
    has_previous = jnp.logical_and(member <= 2, group >= 1)

    def remote(source, target, send_sem, recv_sem, to_group, to_member):
        return pltpu.make_async_remote_copy(
            src_ref=source,
            dst_ref=target,
            send_sem=send_sem,
            recv_sem=recv_sem,
            device_id=(to_group, to_member),
            device_id_type=pl.DeviceIdType.MESH,
        )

    barrier = pltpu.get_barrier_semaphore()

    def greet(to_group, to_member):
        pl.semaphore_signal(
            barrier, inc=1, device_id=(to_group, to_member), device_id_type=pl.DeviceIdType.MESH
        )

    greet(group, sibling)
    greet(group, opposite)
    greet(beside, member)
    greet(along, member)

    @pl.when(has_next)
    def _():
        greet(group + 1, member - 1)

    @pl.when(has_previous)
    def _():
        greet(group - 1, member + 1)

    load_qkv = pltpu.make_async_copy(qkv_hbm, qkv, local_sem.at[0])
    load_weight = pltpu.make_async_copy(weight_hbm, weight.at[member], local_sem.at[1])
    load_latents = pltpu.make_async_copy(latents_hbm, latents, local_sem.at[2])
    load_gates = pltpu.make_async_copy(gates_hbm, gates, local_sem.at[3])
    load_qkv.start()
    load_weight.start()
    load_gates.start()
    load_latents.start()

    pl.semaphore_wait(barrier, 4 + has_next.astype(jnp.int32) + has_previous.astype(jnp.int32))

    sent = []

    def begin(condition, copy):
        sent.append((condition, copy))
        if condition is None:
            copy.start()
        else:
            pl.when(condition)(copy.start)

    def own_block(h):
        return qkv_hbm.at[pl.ds(1, 2), :, pl.ds(h * HEAD, HEAD)]

    def send_opposite(h):
        begin(
            row == 0,
            remote(own_block(h), kv.at[1, h], kv_send.at[0, h], kv_recv.at[1, h], group, opposite),
        )

    def send_near(h):
        begin(
            has_next,
            remote(
                own_block(h), kv.at[2, h], kv_send.at[1, h], kv_recv.at[2, h], group + 1, member - 1
            ),
        )
        begin(
            core == 0,
            remote(own_block(h), kv.at[0, h], kv_send.at[2, h], kv_recv.at[0, h], group, sibling),
        )

    mine = group % 4
    quarters = (
        mine,
        mine + 1 - 2 * (mine % 2),
        mine + 2 - 4 * (mine // 2),
        3 - mine,
    )

    def cut(k):
        return pl.ds(pl.multiple_of((2 * quarters[k // 2] + k % 2) * piece, 16), piece)

    def send_piece(k):
        begin(
            None,
            remote(
                weight_hbm.at[cut(k)],
                weight.at[member, cut(k)],
                w_send.at[k],
                w_recv.at[k],
                group,
                opposite,
            ),
        )

    def send_sibling():
        begin(
            None,
            remote(weight_hbm, weight.at[member], w_send.at[2], w_recv.at[8], group, sibling),
        )

    def arrived(target, sem):
        remote(target, target, w_send.at[0], sem, group, sibling).wait_recv()

    def take_piece(k):
        block = weight.at[opposite, cut(k)]
        arrived(block, w_recv.at[k])

        def pass_on(sem, into, to_group, to_member):
            begin(None, remote(block, block, w_pass.at[sem], w_recv.at[into], to_group, to_member))

        if k < 2:
            pass_on(8 + k, 2 + k, beside, member)
            pass_on(10 + k, 4 + k, along, member)
        if k == 3:
            pass_on(12, 7, along, member)
        if k == 4:
            pass_on(13, 6, beside, member)
        pass_on(k, 9 + k, group, sibling)

    scale = (HEAD ** -0.5) * math.log2(math.e)

    def own_head(index, h):
        return qkv[index, :, h * HEAD : (h + 1) * HEAD]

    def scores_of(h, keys):
        return (
            lax.dot_general(
                keys, own_head(0, h), (((1,), (1,)), ((), ())), preferred_element_type=jnp.float32
            )
            * scale
        )

    def mix(values, weights):
        return lax.dot_general(
            values,
            weights.astype(jnp.bfloat16),
            (((0,), (0,)), ((), ())),
            preferred_element_type=jnp.float32,
        )

    def start_head(h):
        scores = scores_of(h, own_head(1, h))
        row_top = jnp.max(scores, axis=0, keepdims=True)
        weights = jnp.exp2(scores - row_top)
        top[h] = row_top
        total[h] = jnp.sum(weights, axis=0, keepdims=True)
        acc[h] = mix(own_head(2, h), weights)

    def add_frame(h, slot):
        scores = scores_of(h, kv[slot, h, 0])
        old_top = top[h]
        row_top = jnp.maximum(old_top, jnp.max(scores, axis=0, keepdims=True))
        weights = jnp.exp2(scores - row_top)
        shrink = jnp.exp2(old_top - row_top)
        top[h] = row_top
        total[h] = total[h] * shrink + jnp.sum(weights, axis=0, keepdims=True)
        acc[h] = acc[h] * shrink + mix(kv[slot, h, 1], weights)

    order = ((3, 1, 3, 1), (1, 3, 2, 2), (2, 2, 1, 3))

    def place_of(j):
        back = by_member(member, order[j])
        return back - 1, jnp.logical_or(group >= 1, member >= back)

    def receive(j, h):
        slot, exists = place_of(j)
        block = kv.at[slot, h]
        pl.when(exists)(lambda: arrived(block, kv_recv.at[slot, h]))
        if j == 0:
            begin(
                jnp.logical_and(exists, member == 2),
                remote(block, kv.at[0, h], kv_pass.at[0, h], kv_recv.at[0, h], group, opposite),
            )
        if j == 1:
            into = by_member(member, (1, 1, 2, 0))
            begin(
                exists,
                remote(
                    block, kv.at[into, h], kv_pass.at[1, h], kv_recv.at[into, h], group, sibling
                ),
            )

    def attend_frame(j, h):
        slot, exists = place_of(j)
        pl.when(exists)(lambda: add_frame(h, slot))

    def finish_head(h):
        attended[:, h * HEAD : (h + 1) * HEAD] = jnp.transpose(acc[h] / total[h]).astype(jnp.bfloat16)

    send_piece(0)
    send_piece(1)
    for h in range(heads):
        send_near(h)
    send_opposite(0)
    send_opposite(1)
    send_sibling()

    load_qkv.wait()
    start_head(0)
    receive(0, 0)
    start_head(1)
    receive(0, 1)
    take_piece(0)
    for h in range(2, heads - 1):
        send_opposite(h)
    start_head(2)
    receive(0, 2)
    take_piece(1)
    send_opposite(heads - 1)
    for h in range(3, heads):
        start_head(h)
        receive(0, h)
    attend_frame(0, 0)
    take_piece(2)
    take_piece(4)
    attend_frame(0, 1)
    take_piece(3)
    take_piece(5)
    for h in range(2, heads):
        attend_frame(0, h)
    load_gates.wait()
    step_index = lax.broadcasted_iota(jnp.int32, gates.shape, 0)
    gate_row[...] = jnp.sum(
        jnp.where(step_index == steps_ref[member], gates[...], 0.0), axis=0, keepdims=True
    )
    for h in range(heads):
        receive(1, h)
        if h >= 1:
            receive(2, h - 1)
        if h < 2:
            take_piece(6 + h)
        attend_frame(1, h)
        if h >= 1:
            attend_frame(2, h - 1)
            finish_head(h - 1)
    receive(2, heads - 1)
    attend_frame(2, heads - 1)
    finish_head(heads - 1)

    def project(owner, start, width):
        place = pl.ds(pl.multiple_of(owner * columns + start, 128), width)
        branch = jnp.dot(
            attended[...],
            weight[owner, :, pl.ds(start, width)],
            preferred_element_type=jnp.float32,
        )
        out[:, place] = (
            latents[:, place].astype(jnp.float32) + gate_row[:, place] * branch
        ).astype(jnp.bfloat16)

    load_weight.wait()
    load_latents.wait()
    project(member, 0, half)
    project(member, half, half)
    arrived(weight.at[sibling], w_recv.at[8])
    project(sibling, 0, half)
    project(sibling, half, half)
    project(opposite, 0, half)
    project(opposite, half, half)
    for k in range(8):
        arrived(weight.at[far, cut(k)], w_recv.at[9 + k])
    project(far, 0, half)
    project(far, half, half)

    for condition, copy in sent:
        if condition is None:
            copy.wait_send()
        else:
            pl.when(condition)(copy.wait_send)


def frame_body(latents, projected, out_weight, gate_table, timesteps, groups):
    rows, width = latents.shape
    inner, columns = out_weight.shape
    heads = inner // HEAD
    qkv = projected.transpose(1, 0, 2)
    in_hbm = pl.BlockSpec(memory_space=pltpu.HBM)
    return pl.pallas_call(
        functools.partial(frame_kernel, groups),
        out_shape=pltpu.VMEM((rows, width), jnp.bfloat16),
        in_specs=[pl.BlockSpec(memory_space=pltpu.SMEM)] + [in_hbm] * 4,
        out_specs=pl.BlockSpec(memory_space=pltpu.VMEM),
        scratch_shapes=[
            pltpu.VMEM((3, rows, inner), jnp.bfloat16),
            pltpu.VMEM((3, heads, 2, rows, HEAD), jnp.bfloat16),
            pltpu.VMEM((4, inner, columns), jnp.bfloat16),
            pltpu.VMEM((rows, width), jnp.bfloat16),
            pltpu.VMEM(gate_table.shape, jnp.float32),
            pltpu.VMEM((1, width), jnp.float32),
            pltpu.VMEM((heads, 1, rows), jnp.float32),
            pltpu.VMEM((heads, 1, rows), jnp.float32),
            pltpu.VMEM((heads, HEAD, rows), jnp.float32),
            pltpu.VMEM((rows, inner), jnp.bfloat16),
            pltpu.SemaphoreType.DMA((4,)),
            pltpu.SemaphoreType.DMA((3, heads)),
            pltpu.SemaphoreType.DMA((2, heads)),
            pltpu.SemaphoreType.DMA((3, heads)),
            pltpu.SemaphoreType.DMA((3,)),
            pltpu.SemaphoreType.DMA((14,)),
            pltpu.SemaphoreType.DMA((17,)),
        ],
        compiler_params=pltpu.CompilerParams(
            collective_id=0, has_side_effects=True, vmem_limit_bytes=56 * 1024 * 1024
        ),
        cost_estimate=pl.CostEstimate(
            flops=2 * rows * inner * (8 * rows + width),
            bytes_accessed=4 * rows * width + 2 * inner * width,
            transcendentals=4 * heads * rows * rows,
        ),
    )(timesteps, latents, qkv, out_weight, gate_table)


def solution(mesh):
    in_specs = (
        P(("tm", "fsdp"), None),
        P(("tm", "fsdp"), None, None),
        P(None, "fsdp"),
        P(),
        P("tm"),
    )
    out_specs = P(("tm", "fsdp"), None)
    groups, members = mesh.shape["tm"], mesh.shape["fsdp"]

    def local(latents, projected, out_weight, gate_table, timesteps):
        one_frame_each = latents.shape[0] == FRAME_TOK and timesteps.shape[0] == members
        if one_frame_each and members == 4 and groups % 4 == 0:
            return frame_body(latents, projected, out_weight, gate_table, timesteps, groups)
        return body(latents, projected, out_weight, gate_table, timesteps)

    return jax.shard_map(local, mesh=mesh, in_specs=in_specs, out_specs=out_specs, check_vma=False)
```

```python
import functools
import math

import jax
import jax.numpy as jnp
from jax import lax
from jax.experimental import pallas as pl
from jax.experimental.pallas import tpu as pltpu
from jax.sharding import PartitionSpec as P

FRAME_TOK = 256


def passed_along(value, axis, steps):
    count = lax.axis_size(axis)
    initial, last = (max(0, -steps), min(count, count - steps))
    return lax.ppermute(value, axis, [(source, source + steps) for source in range(initial, last)])


def attend(queries, extended, first_frame, frame_count):
    pair_rows = 2 * FRAME_TOK
    key_count = 5 * FRAME_TOK
    score_scale = queries.shape[1] ** (-0.5)
    row_frame = jnp.arange(pair_rows, dtype=jnp.int32) // FRAME_TOK
    col_frame = jnp.arange(key_count, dtype=jnp.int32) // FRAME_TOK

    def frame_pair(pair_index):
        offset = pair_index * pair_rows
        query_block = lax.dynamic_slice_in_dim(queries, offset, pair_rows, 0)
        window = lax.dynamic_slice_in_dim(extended, offset, key_count, 0)
        key_block = window[:, 0]
        value_block = window[:, 1]
        scores = (
            lax.dot_general(
                query_block, key_block, (((1,), (1,)), ((), ())), preferred_element_type=jnp.float32
            )
            * score_scale
        )
        distance = col_frame[None, :] - row_frame[:, None]
        existing = first_frame + 2 * pair_index + col_frame - 3 >= 0
        allowed = (distance >= 0) & (distance <= 3) & existing[None, :]
        scores = jnp.where(allowed, scores, -1e30)
        row_max = jnp.max(scores, axis=-1, keepdims=True)
        weights = jnp.exp(scores - row_max)
        row_sum = jnp.sum(weights, axis=-1, keepdims=True)
        probability = (weights / row_sum).astype(jnp.bfloat16)
        return jnp.dot(probability, value_block, preferred_element_type=jnp.float32).astype(
            jnp.bfloat16
        )

    blocks = lax.map(frame_pair, jnp.arange(frame_count // 2, dtype=jnp.int32))
    return blocks.reshape(frame_count * FRAME_TOK, queries.shape[1])


def body(latents, projected, out_weight, gate_table, timesteps):
    row_count = latents.shape[0]
    frame_count = timesteps.shape[0]
    group_tokens = frame_count * FRAME_TOK
    head_view = lax.all_to_all(projected, "fsdp", split_axis=2, concat_axis=0, tiled=True)
    queries = head_view[:, 0]
    key_values = head_view[:, 1:3]
    trailing = passed_along(key_values[group_tokens - 3 * FRAME_TOK :], "tm", 1)
    extended = jnp.concatenate([trailing, key_values], axis=0)
    first_frame = lax.axis_index("tm") * frame_count
    attended = attend(queries, extended, first_frame, frame_count)
    gathered_heads = lax.all_to_all(attended, "fsdp", split_axis=0, concat_axis=1, tiled=True)
    update = jnp.dot(
        gathered_heads,
        lax.all_gather(out_weight, "fsdp", axis=1, tiled=True),
        preferred_element_type=jnp.float32,
    )
    step_count = gate_table.shape[0]
    step_onehot = (timesteps[:, None] == jnp.arange(step_count, dtype=jnp.int32)[None, :]).astype(
        jnp.float32
    )
    frame_gates = jnp.dot(step_onehot, gate_table, precision=lax.Precision.HIGHEST)
    row_frame = (
        lax.axis_index("fsdp") * row_count + jnp.arange(row_count, dtype=jnp.int32)
    ) // FRAME_TOK
    row_onehot = (row_frame[:, None] == jnp.arange(frame_count, dtype=jnp.int32)[None, :]).astype(
        jnp.float32
    )
    row_gates = jnp.dot(row_onehot, frame_gates, precision=lax.Precision.HIGHEST)
    return (latents.astype(jnp.float32) + row_gates * update).astype(jnp.bfloat16)


HEAD = 128


def by_member(member, values):
    row, core = member // 2, member % 2
    v0, v1, v2, v3 = values
    return v0 + (v1 - v0) * core + (v2 - v0) * row + (v3 - v2 - v1 + v0) * core * row


def frame_kernel(
    groups,
    steps_ref,
    latents_hbm,
    qkv_hbm,
    weight_hbm,
    gates_hbm,
    out,
    qkv,
    kv,
    weight,
    latents,
    gates,
    gate_row,
    top,
    total,
    acc,
    attended,
    local_sem,
    kv_send,
    kv_pass,
    kv_recv,
    w_send,
    w_pass,
    w_recv,
):
    heads = kv.shape[1]
    columns = weight.shape[2]
    half = columns // 2
    piece = weight.shape[1] // 8
    group, member = lax.axis_index("tm"), lax.axis_index("fsdp")
    row, core = member // 2, member % 2
    beside = group + 1 - 2 * (group % 2)
    along = group + 2 - 4 * ((group // 2) % 2)
    sibling = member + 1 - 2 * core
    opposite = member + 2 - 4 * row
    far = 3 - member
    has_next = jnp.logical_and(member >= 1, group < groups - 1)
    has_previous = jnp.logical_and(member <= 2, group >= 1)

    def remote(source, target, send_sem, recv_sem, to_group, to_member):
        return pltpu.make_async_remote_copy(
            src_ref=source,
            dst_ref=target,
            send_sem=send_sem,
            recv_sem=recv_sem,
            device_id=(to_group, to_member),
            device_id_type=pl.DeviceIdType.MESH,
        )

    barrier = pltpu.get_barrier_semaphore()

    def greet(to_group, to_member):
        pl.semaphore_signal(
            barrier, inc=1, device_id=(to_group, to_member), device_id_type=pl.DeviceIdType.MESH
        )

    greet(group, sibling)
    greet(group, opposite)
    greet(beside, member)
    greet(along, member)

    @pl.when(has_next)
    def _():
        greet(group + 1, member - 1)

    @pl.when(has_previous)
    def _():
        greet(group - 1, member + 1)

    load_heads = [
        pltpu.make_async_copy(
            qkv_hbm.at[:, :, pl.ds(h * HEAD, HEAD)], qkv.at[h], local_sem.at[3 + h]
        )
        for h in range(heads)
    ]
    load_weight = pltpu.make_async_copy(weight_hbm, weight.at[member], local_sem.at[0])
    load_latents = pltpu.make_async_copy(latents_hbm, latents, local_sem.at[1])
    load_gates = pltpu.make_async_copy(gates_hbm, gates, local_sem.at[2])
    for load in load_heads:
        load.start()
    load_weight.start()
    load_gates.start()
    load_latents.start()

    pl.semaphore_wait(barrier, 4 + has_next.astype(jnp.int32) + has_previous.astype(jnp.int32))

    sent = []

    def begin(condition, copy):
        sent.append((condition, copy))
        if condition is None:
            copy.start()
        else:
            pl.when(condition)(copy.start)

    def own_block(h):
        return qkv.at[h, pl.ds(1, 2)]

    def send_opposite(h):
        begin(
            row == 0,
            remote(own_block(h), kv.at[1, h], kv_send.at[0, h], kv_recv.at[1, h], group, opposite),
        )

    def send_near(h):
        begin(
            has_next,
            remote(
                own_block(h), kv.at[2, h], kv_send.at[1, h], kv_recv.at[2, h], group + 1, member - 1
            ),
        )
        begin(
            core == 0,
            remote(own_block(h), kv.at[0, h], kv_send.at[2, h], kv_recv.at[0, h], group, sibling),
        )

    mine = group % 4
    quarters = (
        mine,
        mine + 1 - 2 * (mine % 2),
        mine + 2 - 4 * (mine // 2),
        3 - mine,
    )

    def cut(k):
        return pl.ds(pl.multiple_of((2 * quarters[k // 2] + k % 2) * piece, 16), piece)

    def send_piece(k):
        begin(
            None,
            remote(
                weight_hbm.at[cut(k)],
                weight.at[member, cut(k)],
                w_send.at[k],
                w_recv.at[k],
                group,
                opposite,
            ),
        )

    def send_sibling():
        begin(
            None,
            remote(weight_hbm, weight.at[member], w_send.at[2], w_recv.at[8], group, sibling),
        )

    def arrived(target, sem):
        remote(target, target, w_send.at[0], sem, group, sibling).wait_recv()

    def take_piece(k):
        block = weight.at[opposite, cut(k)]
        arrived(block, w_recv.at[k])

        def pass_on(sem, into, to_group, to_member):
            begin(None, remote(block, block, w_pass.at[sem], w_recv.at[into], to_group, to_member))

        if k < 2:
            pass_on(8 + k, 2 + k, beside, member)
            pass_on(10 + k, 4 + k, along, member)
        if k == 3:
            pass_on(12, 7, along, member)
        if k == 4:
            pass_on(13, 6, beside, member)
        pass_on(k, 9 + k, group, sibling)

    scale = (HEAD ** -0.5) * math.log2(math.e)

    def own_head(index, h):
        return qkv[h, index]

    def scores_of(h, keys):
        return (
            lax.dot_general(
                keys, own_head(0, h), (((1,), (1,)), ((), ())), preferred_element_type=jnp.float32
            )
            * scale
        )

    def mix(values, weights):
        return lax.dot_general(
            values,
            weights.astype(jnp.bfloat16),
            (((0,), (0,)), ((), ())),
            preferred_element_type=jnp.float32,
        )

    def start_head(h):
        scores = scores_of(h, own_head(1, h))
        row_top = jnp.max(scores, axis=0, keepdims=True)
        weights = jnp.exp2(scores - row_top)
        top[h] = row_top
        total[h] = jnp.sum(weights, axis=0, keepdims=True)
        acc[h] = mix(own_head(2, h), weights)

    def add_frame(h, slot):
        scores = scores_of(h, kv[slot, h, 0])
        old_top = top[h]
        row_top = jnp.maximum(old_top, jnp.max(scores, axis=0, keepdims=True))
        weights = jnp.exp2(scores - row_top)
        shrink = jnp.exp2(old_top - row_top)
        top[h] = row_top
        total[h] = total[h] * shrink + jnp.sum(weights, axis=0, keepdims=True)
        acc[h] = acc[h] * shrink + mix(kv[slot, h, 1], weights)

    order = ((3, 1, 3, 1), (1, 3, 2, 2), (2, 2, 1, 3))

    def place_of(j):
        back = by_member(member, order[j])
        return back - 1, jnp.logical_or(group >= 1, member >= back)

    def receive(j, h):
        slot, exists = place_of(j)
        block = kv.at[slot, h]
        pl.when(exists)(lambda: arrived(block, kv_recv.at[slot, h]))
        if j == 0:
            begin(
                jnp.logical_and(exists, member == 2),
                remote(block, kv.at[0, h], kv_pass.at[0, h], kv_recv.at[0, h], group, opposite),
            )
        if j == 1:
            into = by_member(member, (1, 1, 2, 0))
            begin(
                exists,
                remote(
                    block, kv.at[into, h], kv_pass.at[1, h], kv_recv.at[into, h], group, sibling
                ),
            )

    def attend_frame(j, h):
        slot, exists = place_of(j)
        pl.when(exists)(lambda: add_frame(h, slot))

    def finish_head(h):
        attended[:, h * HEAD : (h + 1) * HEAD] = jnp.transpose(acc[h] / total[h]).astype(jnp.bfloat16)

    for h in range(heads):
        load_heads[h].wait()
        send_opposite(h)
        if h < 2:
            send_piece(h)
        send_near(h)
    send_sibling()

    start_head(0)
    receive(0, 0)
    start_head(1)
    receive(0, 1)
    take_piece(0)
    start_head(2)
    receive(0, 2)
    take_piece(1)
    for h in range(3, heads):
        start_head(h)
        receive(0, h)
    attend_frame(0, 0)
    take_piece(2)
    take_piece(4)
    attend_frame(0, 1)
    take_piece(3)
    take_piece(5)
    for h in range(2, heads):
        attend_frame(0, h)
    load_gates.wait()
    step_index = lax.broadcasted_iota(jnp.int32, gates.shape, 0)
    gate_row[...] = jnp.sum(
        jnp.where(step_index == steps_ref[member], gates[...], 0.0), axis=0, keepdims=True
    )
    for h in range(heads):
        receive(1, h)
        if h >= 1:
            receive(2, h - 1)
        if h < 2:
            take_piece(6 + h)
        attend_frame(1, h)
        if h >= 1:
            attend_frame(2, h - 1)
            finish_head(h - 1)
    receive(2, heads - 1)
    attend_frame(2, heads - 1)
    finish_head(heads - 1)

    def project(owner, start, width):
        place = pl.ds(pl.multiple_of(owner * columns + start, 128), width)
        branch = jnp.dot(
            attended[...],
            weight[owner, :, pl.ds(start, width)],
            preferred_element_type=jnp.float32,
        )
        out[:, place] = (
            latents[:, place].astype(jnp.float32) + gate_row[:, place] * branch
        ).astype(jnp.bfloat16)

    load_weight.wait()
    load_latents.wait()
    project(member, 0, half)
    project(member, half, half)
    arrived(weight.at[sibling], w_recv.at[8])
    project(sibling, 0, half)
    project(sibling, half, half)
    project(opposite, 0, half)
    project(opposite, half, half)
    for k in range(8):
        arrived(weight.at[far, cut(k)], w_recv.at[9 + k])
    project(far, 0, half)
    project(far, half, half)

    for condition, copy in sent:
        if condition is None:
            copy.wait_send()
        else:
            pl.when(condition)(copy.wait_send)


def frame_body(latents, projected, out_weight, gate_table, timesteps, groups):
    rows, width = latents.shape
    inner, columns = out_weight.shape
    heads = inner // HEAD
    qkv = projected.transpose(1, 0, 2)
    in_hbm = pl.BlockSpec(memory_space=pltpu.HBM)
    return pl.pallas_call(
        functools.partial(frame_kernel, groups),
        out_shape=pltpu.VMEM((rows, width), jnp.bfloat16),
        in_specs=[pl.BlockSpec(memory_space=pltpu.SMEM)] + [in_hbm] * 4,
        out_specs=pl.BlockSpec(memory_space=pltpu.VMEM),
        scratch_shapes=[
            pltpu.VMEM((heads, 3, rows, HEAD), jnp.bfloat16),
            pltpu.VMEM((3, heads, 2, rows, HEAD), jnp.bfloat16),
            pltpu.VMEM((4, inner, columns), jnp.bfloat16),
            pltpu.VMEM((rows, width), jnp.bfloat16),
            pltpu.VMEM(gate_table.shape, jnp.float32),
            pltpu.VMEM((1, width), jnp.float32),
            pltpu.VMEM((heads, 1, rows), jnp.float32),
            pltpu.VMEM((heads, 1, rows), jnp.float32),
            pltpu.VMEM((heads, HEAD, rows), jnp.float32),
            pltpu.VMEM((rows, inner), jnp.bfloat16),
            pltpu.SemaphoreType.DMA((3 + heads,)),
            pltpu.SemaphoreType.DMA((3, heads)),
            pltpu.SemaphoreType.DMA((2, heads)),
            pltpu.SemaphoreType.DMA((3, heads)),
            pltpu.SemaphoreType.DMA((3,)),
            pltpu.SemaphoreType.DMA((14,)),
            pltpu.SemaphoreType.DMA((17,)),
        ],
        compiler_params=pltpu.CompilerParams(
            collective_id=0, has_side_effects=True, vmem_limit_bytes=56 * 1024 * 1024
        ),
        cost_estimate=pl.CostEstimate(
            flops=2 * rows * inner * (8 * rows + width),
            bytes_accessed=4 * rows * width + 2 * inner * width,
            transcendentals=4 * heads * rows * rows,
        ),
    )(timesteps, latents, qkv, out_weight, gate_table)


def solution(mesh):
    in_specs = (
        P(("tm", "fsdp"), None),
        P(("tm", "fsdp"), None, None),
        P(None, "fsdp"),
        P(),
        P("tm"),
    )
    out_specs = P(("tm", "fsdp"), None)
    groups, members = mesh.shape["tm"], mesh.shape["fsdp"]

    def local(latents, projected, out_weight, gate_table, timesteps):
        one_frame_each = latents.shape[0] == FRAME_TOK and timesteps.shape[0] == members
        if one_frame_each and members == 4 and groups % 4 == 0:
            return frame_body(latents, projected, out_weight, gate_table, timesteps, groups)
        return body(latents, projected, out_weight, gate_table, timesteps)

    return jax.shard_map(local, mesh=mesh, in_specs=in_specs, out_specs=out_specs, check_vma=False)
```

```python
import functools
import math

import jax
import jax.numpy as jnp
from jax import lax
from jax.experimental import pallas as pl
from jax.experimental.pallas import tpu as pltpu
from jax.sharding import PartitionSpec as P

FRAME_TOK = 256


def passed_along(value, axis, steps):
    count = lax.axis_size(axis)
    initial, last = (max(0, -steps), min(count, count - steps))
    return lax.ppermute(value, axis, [(source, source + steps) for source in range(initial, last)])


def attend(queries, extended, first_frame, frame_count):
    pair_rows = 2 * FRAME_TOK
    key_count = 5 * FRAME_TOK
    score_scale = queries.shape[1] ** (-0.5)
    row_frame = jnp.arange(pair_rows, dtype=jnp.int32) // FRAME_TOK
    col_frame = jnp.arange(key_count, dtype=jnp.int32) // FRAME_TOK

    def frame_pair(pair_index):
        offset = pair_index * pair_rows
        query_block = lax.dynamic_slice_in_dim(queries, offset, pair_rows, 0)
        window = lax.dynamic_slice_in_dim(extended, offset, key_count, 0)
        key_block = window[:, 0]
        value_block = window[:, 1]
        scores = (
            lax.dot_general(
                query_block, key_block, (((1,), (1,)), ((), ())), preferred_element_type=jnp.float32
            )
            * score_scale
        )
        distance = col_frame[None, :] - row_frame[:, None]
        existing = first_frame + 2 * pair_index + col_frame - 3 >= 0
        allowed = (distance >= 0) & (distance <= 3) & existing[None, :]
        scores = jnp.where(allowed, scores, -1e30)
        row_max = jnp.max(scores, axis=-1, keepdims=True)
        weights = jnp.exp(scores - row_max)
        row_sum = jnp.sum(weights, axis=-1, keepdims=True)
        probability = (weights / row_sum).astype(jnp.bfloat16)
        return jnp.dot(probability, value_block, preferred_element_type=jnp.float32).astype(
            jnp.bfloat16
        )

    blocks = lax.map(frame_pair, jnp.arange(frame_count // 2, dtype=jnp.int32))
    return blocks.reshape(frame_count * FRAME_TOK, queries.shape[1])


def body(latents, projected, out_weight, gate_table, timesteps):
    row_count = latents.shape[0]
    frame_count = timesteps.shape[0]
    group_tokens = frame_count * FRAME_TOK
    head_view = lax.all_to_all(projected, "fsdp", split_axis=2, concat_axis=0, tiled=True)
    queries = head_view[:, 0]
    key_values = head_view[:, 1:3]
    trailing = passed_along(key_values[group_tokens - 3 * FRAME_TOK :], "tm", 1)
    extended = jnp.concatenate([trailing, key_values], axis=0)
    first_frame = lax.axis_index("tm") * frame_count
    attended = attend(queries, extended, first_frame, frame_count)
    gathered_heads = lax.all_to_all(attended, "fsdp", split_axis=0, concat_axis=1, tiled=True)
    update = jnp.dot(
        gathered_heads,
        lax.all_gather(out_weight, "fsdp", axis=1, tiled=True),
        preferred_element_type=jnp.float32,
    )
    step_count = gate_table.shape[0]
    step_onehot = (timesteps[:, None] == jnp.arange(step_count, dtype=jnp.int32)[None, :]).astype(
        jnp.float32
    )
    frame_gates = jnp.dot(step_onehot, gate_table, precision=lax.Precision.HIGHEST)
    row_frame = (
        lax.axis_index("fsdp") * row_count + jnp.arange(row_count, dtype=jnp.int32)
    ) // FRAME_TOK
    row_onehot = (row_frame[:, None] == jnp.arange(frame_count, dtype=jnp.int32)[None, :]).astype(
        jnp.float32
    )
    row_gates = jnp.dot(row_onehot, frame_gates, precision=lax.Precision.HIGHEST)
    return (latents.astype(jnp.float32) + row_gates * update).astype(jnp.bfloat16)


HEAD = 128


def by_member(member, values):
    row, core = member // 2, member % 2
    v0, v1, v2, v3 = values
    return v0 + (v1 - v0) * core + (v2 - v0) * row + (v3 - v2 - v1 + v0) * core * row


def frame_kernel(
    groups,
    steps_ref,
    latents_hbm,
    qkv_hbm,
    weight_hbm,
    gates_hbm,
    out,
    qkv,
    kv,
    relay,
    weight,
    latents,
    gates,
    gate_row,
    top,
    total,
    acc,
    attended,
    local_sem,
    kv_send,
    kv_pass,
    kv_recv,
    w_send,
    w_pass,
    w_recv,
    relay_send,
    relay_pass,
    relay_recv,
):
    heads = kv.shape[1]
    columns = weight.shape[2]
    half = columns // 2
    piece = weight.shape[1] // 8
    group, member = lax.axis_index("tm"), lax.axis_index("fsdp")
    row, core = member // 2, member % 2
    beside = group + 1 - 2 * (group % 2)
    along = group + 2 - 4 * ((group // 2) % 2)
    sibling = member + 1 - 2 * core
    opposite = member + 2 - 4 * row
    far = 3 - member
    has_next = jnp.logical_and(member >= 1, group < groups - 1)
    has_previous = jnp.logical_and(member <= 2, group >= 1)

    by_way = heads // 2
    relays = jnp.logical_and(member == 0, group < groups - 1)
    has_relay = jnp.logical_and(member == 1, group >= 1)

    def remote(source, target, send_sem, recv_sem, to_group, to_member):
        return pltpu.make_async_remote_copy(
            src_ref=source,
            dst_ref=target,
            send_sem=send_sem,
            recv_sem=recv_sem,
            device_id=(to_group, to_member),
            device_id_type=pl.DeviceIdType.MESH,
        )

    barrier = pltpu.get_barrier_semaphore()

    def greet(to_group, to_member):
        pl.semaphore_signal(
            barrier, inc=1, device_id=(to_group, to_member), device_id_type=pl.DeviceIdType.MESH
        )

    greet(group, sibling)
    greet(group, opposite)
    greet(beside, member)
    greet(along, member)

    @pl.when(has_next)
    def _():
        greet(group + 1, member - 1)

    @pl.when(has_previous)
    def _():
        greet(group - 1, member + 1)

    @pl.when(relays)
    def _():
        greet(group + 1, 1)

    @pl.when(has_relay)
    def _():
        greet(group - 1, 0)

    load_heads = [
        pltpu.make_async_copy(
            qkv_hbm.at[:, :, pl.ds(h * HEAD, HEAD)], qkv.at[h], local_sem.at[3 + h]
        )
        for h in range(heads)
    ]
    load_weight = pltpu.make_async_copy(weight_hbm, weight.at[member], local_sem.at[0])
    load_latents = pltpu.make_async_copy(latents_hbm, latents, local_sem.at[1])
    load_gates = pltpu.make_async_copy(gates_hbm, gates, local_sem.at[2])
    for load in load_heads:
        load.start()
    load_weight.start()
    load_gates.start()
    load_latents.start()

    peers = 4
    for present in (has_next, has_previous, relays, has_relay):
        peers = peers + present.astype(jnp.int32)
    pl.semaphore_wait(barrier, peers)

    sent = []

    def begin(condition, copy):
        sent.append((condition, copy))
        if condition is None:
            copy.start()
        else:
            pl.when(condition)(copy.start)

    def own_block(h):
        return qkv.at[h, pl.ds(1, 2)]

    def send_opposite(h):
        begin(
            row == 0,
            remote(own_block(h), kv.at[1, h], kv_send.at[0, h], kv_recv.at[1, h], group, opposite),
        )

    def send_near(h):
        direct = has_next
        if h < by_way:
            direct = jnp.logical_and(has_next, member != 2)
            begin(
                jnp.logical_and(has_next, member == 2),
                remote(
                    own_block(h), relay.at[h], relay_send.at[h], relay_recv.at[h], group, opposite
                ),
            )
        begin(
            direct,
            remote(
                own_block(h), kv.at[2, h], kv_send.at[1, h], kv_recv.at[2, h], group + 1, member - 1
            ),
        )
        begin(
            core == 0,
            remote(own_block(h), kv.at[0, h], kv_send.at[2, h], kv_recv.at[0, h], group, sibling),
        )

    def pass_relay(h):
        block = relay.at[h]
        pl.when(relays)(lambda: arrived(block, relay_recv.at[h]))
        begin(
            relays,
            remote(block, kv.at[2, h], relay_pass.at[h], kv_recv.at[2, h], group + 1, member + 1),
        )

    mine = group % 4
    quarters = (
        mine,
        mine + 1 - 2 * (mine % 2),
        mine + 2 - 4 * (mine // 2),
        3 - mine,
    )

    def cut(k):
        return pl.ds(pl.multiple_of((2 * quarters[k // 2] + k % 2) * piece, 16), piece)

    def send_piece(k):
        begin(
            None,
            remote(
                weight_hbm.at[cut(k)],
                weight.at[member, cut(k)],
                w_send.at[k],
                w_recv.at[k],
                group,
                opposite,
            ),
        )

    def send_sibling():
        begin(
            None,
            remote(weight_hbm, weight.at[member], w_send.at[2], w_recv.at[8], group, sibling),
        )

    def arrived(target, sem):
        remote(target, target, w_send.at[0], sem, group, sibling).wait_recv()

    def take_piece(k):
        block = weight.at[opposite, cut(k)]
        arrived(block, w_recv.at[k])

        def pass_on(sem, into, to_group, to_member):
            begin(None, remote(block, block, w_pass.at[sem], w_recv.at[into], to_group, to_member))

        if k < 2:
            pass_on(8 + k, 2 + k, beside, member)
            pass_on(10 + k, 4 + k, along, member)
        if k == 3:
            pass_on(12, 7, along, member)
        if k == 4:
            pass_on(13, 6, beside, member)
        pass_on(k, 9 + k, group, sibling)

    scale = (HEAD ** -0.5) * math.log2(math.e)

    def own_head(index, h):
        return qkv[h, index]

    def scores_of(h, keys):
        return (
            lax.dot_general(
                keys, own_head(0, h), (((1,), (1,)), ((), ())), preferred_element_type=jnp.float32
            )
            * scale
        )

    def mix(values, weights):
        return lax.dot_general(
            values,
            weights.astype(jnp.bfloat16),
            (((0,), (0,)), ((), ())),
            preferred_element_type=jnp.float32,
        )

    def start_head(h):
        scores = scores_of(h, own_head(1, h))
        row_top = jnp.max(scores, axis=0, keepdims=True)
        weights = jnp.exp2(scores - row_top)
        top[h] = row_top
        total[h] = jnp.sum(weights, axis=0, keepdims=True)
        acc[h] = mix(own_head(2, h), weights)

    def add_frame(h, slot):
        scores = scores_of(h, kv[slot, h, 0])
        old_top = top[h]
        row_top = jnp.maximum(old_top, jnp.max(scores, axis=0, keepdims=True))
        weights = jnp.exp2(scores - row_top)
        shrink = jnp.exp2(old_top - row_top)
        top[h] = row_top
        total[h] = total[h] * shrink + jnp.sum(weights, axis=0, keepdims=True)
        acc[h] = acc[h] * shrink + mix(kv[slot, h, 1], weights)

    order = ((3, 1, 3, 1), (1, 3, 2, 2), (2, 2, 1, 3))

    def place_of(j):
        back = by_member(member, order[j])
        return back - 1, jnp.logical_or(group >= 1, member >= back)

    def receive(j, h):
        slot, exists = place_of(j)
        block = kv.at[slot, h]
        pl.when(exists)(lambda: arrived(block, kv_recv.at[slot, h]))
        if j == 0:
            begin(
                jnp.logical_and(exists, member == 2),
                remote(block, kv.at[0, h], kv_pass.at[0, h], kv_recv.at[0, h], group, opposite),
            )
        if j == 1:
            into = by_member(member, (1, 1, 2, 0))
            begin(
                exists,
                remote(
                    block, kv.at[into, h], kv_pass.at[1, h], kv_recv.at[into, h], group, sibling
                ),
            )

    def attend_frame(j, h):
        slot, exists = place_of(j)
        pl.when(exists)(lambda: add_frame(h, slot))

    def finish_head(h):
        attended[:, h * HEAD : (h + 1) * HEAD] = jnp.transpose(acc[h] / total[h]).astype(jnp.bfloat16)

    send_piece(0)
    send_piece(1)
    for h in range(heads):
        load_heads[h].wait()
        send_near(h)
    send_opposite(0)
    send_sibling()

    start_head(0)
    start_head(1)
    receive(0, 0)
    take_piece(0)
    for h in range(1, heads - 1):
        send_opposite(h)
    start_head(2)
    receive(0, 1)
    take_piece(1)
    send_opposite(heads - 1)
    for h in range(3, heads):
        start_head(h)
    for h in range(by_way):
        pass_relay(h)
    take_piece(2)
    take_piece(4)
    for h in range(2, heads):
        receive(0, h)
    attend_frame(0, 0)
    take_piece(3)
    take_piece(5)
    receive(1, 0)
    attend_frame(0, 1)
    take_piece(6)
    take_piece(7)
    receive(1, 1)
    for h in range(2, heads):
        attend_frame(0, h)
    load_gates.wait()
    step_index = lax.broadcasted_iota(jnp.int32, gates.shape, 0)
    gate_row[...] = jnp.sum(
        jnp.where(step_index == steps_ref[member], gates[...], 0.0), axis=0, keepdims=True
    )
    for h in range(heads):
        if h >= 2:
            receive(1, h)
        if h >= 1:
            receive(2, h - 1)
        attend_frame(1, h)
        if h >= 1:
            attend_frame(2, h - 1)
            finish_head(h - 1)
    receive(2, heads - 1)
    attend_frame(2, heads - 1)
    finish_head(heads - 1)

    def project(owner, start, width):
        place = pl.ds(pl.multiple_of(owner * columns + start, 128), width)
        branch = jnp.dot(
            attended[...],
            weight[owner, :, pl.ds(start, width)],
            preferred_element_type=jnp.float32,
        )
        out[:, place] = (
            latents[:, place].astype(jnp.float32) + gate_row[:, place] * branch
        ).astype(jnp.bfloat16)

    load_weight.wait()
    load_latents.wait()
    project(member, 0, half)
    project(member, half, half)
    arrived(weight.at[sibling], w_recv.at[8])
    project(sibling, 0, half)
    project(sibling, half, half)
    project(opposite, 0, half)
    project(opposite, half, half)
    for k in range(8):
        arrived(weight.at[far, cut(k)], w_recv.at[9 + k])
    project(far, 0, half)
    project(far, half, half)

    for condition, copy in sent:
        if condition is None:
            copy.wait_send()
        else:
            pl.when(condition)(copy.wait_send)


def frame_body(latents, projected, out_weight, gate_table, timesteps, groups):
    rows, width = latents.shape
    inner, columns = out_weight.shape
    heads = inner // HEAD
    qkv = projected.transpose(1, 0, 2)
    in_hbm = pl.BlockSpec(memory_space=pltpu.HBM)
    return pl.pallas_call(
        functools.partial(frame_kernel, groups),
        out_shape=pltpu.VMEM((rows, width), jnp.bfloat16),
        in_specs=[pl.BlockSpec(memory_space=pltpu.SMEM)] + [in_hbm] * 4,
        out_specs=pl.BlockSpec(memory_space=pltpu.VMEM),
        scratch_shapes=[
            pltpu.VMEM((heads, 3, rows, HEAD), jnp.bfloat16),
            pltpu.VMEM((3, heads, 2, rows, HEAD), jnp.bfloat16),
            pltpu.VMEM((heads // 2, 2, rows, HEAD), jnp.bfloat16),
            pltpu.VMEM((4, inner, columns), jnp.bfloat16),
            pltpu.VMEM((rows, width), jnp.bfloat16),
            pltpu.VMEM(gate_table.shape, jnp.float32),
            pltpu.VMEM((1, width), jnp.float32),
            pltpu.VMEM((heads, 1, rows), jnp.float32),
            pltpu.VMEM((heads, 1, rows), jnp.float32),
            pltpu.VMEM((heads, HEAD, rows), jnp.float32),
            pltpu.VMEM((rows, inner), jnp.bfloat16),
            pltpu.SemaphoreType.DMA((3 + heads,)),
            pltpu.SemaphoreType.DMA((3, heads)),
            pltpu.SemaphoreType.DMA((2, heads)),
            pltpu.SemaphoreType.DMA((3, heads)),
            pltpu.SemaphoreType.DMA((3,)),
            pltpu.SemaphoreType.DMA((14,)),
            pltpu.SemaphoreType.DMA((17,)),
            pltpu.SemaphoreType.DMA((heads // 2,)),
            pltpu.SemaphoreType.DMA((heads // 2,)),
            pltpu.SemaphoreType.DMA((heads // 2,)),
        ],
        compiler_params=pltpu.CompilerParams(
            collective_id=0, has_side_effects=True, vmem_limit_bytes=56 * 1024 * 1024
        ),
        cost_estimate=pl.CostEstimate(
            flops=2 * rows * inner * (8 * rows + width),
            bytes_accessed=4 * rows * width + 2 * inner * width,
            transcendentals=4 * heads * rows * rows,
        ),
    )(timesteps, latents, qkv, out_weight, gate_table)


def solution(mesh):
    in_specs = (
        P(("tm", "fsdp"), None),
        P(("tm", "fsdp"), None, None),
        P(None, "fsdp"),
        P(),
        P("tm"),
    )
    out_specs = P(("tm", "fsdp"), None)
    groups, members = mesh.shape["tm"], mesh.shape["fsdp"]

    def local(latents, projected, out_weight, gate_table, timesteps):
        one_frame_each = latents.shape[0] == FRAME_TOK and timesteps.shape[0] == members
        if one_frame_each and members == 4 and groups % 4 == 0:
            return frame_body(latents, projected, out_weight, gate_table, timesteps, groups)
        return body(latents, projected, out_weight, gate_table, timesteps)

    return jax.shard_map(local, mesh=mesh, in_specs=in_specs, out_specs=out_specs, check_vma=False)
```

```python
import functools
import math

import jax
import jax.numpy as jnp
from jax import lax
from jax.experimental import pallas as pl
from jax.experimental.pallas import tpu as pltpu
from jax.sharding import PartitionSpec as P

FRAME_TOK = 256


def passed_along(value, axis, steps):
    count = lax.axis_size(axis)
    initial, last = (max(0, -steps), min(count, count - steps))
    return lax.ppermute(value, axis, [(source, source + steps) for source in range(initial, last)])


def attend(queries, extended, first_frame, frame_count):
    pair_rows = 2 * FRAME_TOK
    key_count = 5 * FRAME_TOK
    score_scale = queries.shape[1] ** (-0.5)
    row_frame = jnp.arange(pair_rows, dtype=jnp.int32) // FRAME_TOK
    col_frame = jnp.arange(key_count, dtype=jnp.int32) // FRAME_TOK

    def frame_pair(pair_index):
        offset = pair_index * pair_rows
        query_block = lax.dynamic_slice_in_dim(queries, offset, pair_rows, 0)
        window = lax.dynamic_slice_in_dim(extended, offset, key_count, 0)
        key_block = window[:, 0]
        value_block = window[:, 1]
        scores = (
            lax.dot_general(
                query_block, key_block, (((1,), (1,)), ((), ())), preferred_element_type=jnp.float32
            )
            * score_scale
        )
        distance = col_frame[None, :] - row_frame[:, None]
        existing = first_frame + 2 * pair_index + col_frame - 3 >= 0
        allowed = (distance >= 0) & (distance <= 3) & existing[None, :]
        scores = jnp.where(allowed, scores, -1e30)
        row_max = jnp.max(scores, axis=-1, keepdims=True)
        weights = jnp.exp(scores - row_max)
        row_sum = jnp.sum(weights, axis=-1, keepdims=True)
        probability = (weights / row_sum).astype(jnp.bfloat16)
        return jnp.dot(probability, value_block, preferred_element_type=jnp.float32).astype(
            jnp.bfloat16
        )

    blocks = lax.map(frame_pair, jnp.arange(frame_count // 2, dtype=jnp.int32))
    return blocks.reshape(frame_count * FRAME_TOK, queries.shape[1])


def body(latents, projected, out_weight, gate_table, timesteps):
    row_count = latents.shape[0]
    frame_count = timesteps.shape[0]
    group_tokens = frame_count * FRAME_TOK
    head_view = lax.all_to_all(projected, "fsdp", split_axis=2, concat_axis=0, tiled=True)
    queries = head_view[:, 0]
    key_values = head_view[:, 1:3]
    trailing = passed_along(key_values[group_tokens - 3 * FRAME_TOK :], "tm", 1)
    extended = jnp.concatenate([trailing, key_values], axis=0)
    first_frame = lax.axis_index("tm") * frame_count
    attended = attend(queries, extended, first_frame, frame_count)
    gathered_heads = lax.all_to_all(attended, "fsdp", split_axis=0, concat_axis=1, tiled=True)
    update = jnp.dot(
        gathered_heads,
        lax.all_gather(out_weight, "fsdp", axis=1, tiled=True),
        preferred_element_type=jnp.float32,
    )
    step_count = gate_table.shape[0]
    step_onehot = (timesteps[:, None] == jnp.arange(step_count, dtype=jnp.int32)[None, :]).astype(
        jnp.float32
    )
    frame_gates = jnp.dot(step_onehot, gate_table, precision=lax.Precision.HIGHEST)
    row_frame = (
        lax.axis_index("fsdp") * row_count + jnp.arange(row_count, dtype=jnp.int32)
    ) // FRAME_TOK
    row_onehot = (row_frame[:, None] == jnp.arange(frame_count, dtype=jnp.int32)[None, :]).astype(
        jnp.float32
    )
    row_gates = jnp.dot(row_onehot, frame_gates, precision=lax.Precision.HIGHEST)
    return (latents.astype(jnp.float32) + row_gates * update).astype(jnp.bfloat16)


HEAD = 128


def by_member(member, values):
    row, core = member // 2, member % 2
    v0, v1, v2, v3 = values
    return v0 + (v1 - v0) * core + (v2 - v0) * row + (v3 - v2 - v1 + v0) * core * row


def frame_kernel(
    groups,
    steps_ref,
    latents_hbm,
    qkv_hbm,
    weight_hbm,
    gates_hbm,
    out,
    qkv,
    kv,
    relay,
    weight,
    latents,
    gates,
    gate_row,
    top,
    total,
    acc,
    attended,
    partial,
    local_sem,
    kv_send,
    kv_pass,
    kv_recv,
    w_send,
    w_pass,
    w_recv,
    relay_send,
    relay_pass,
    relay_recv,
):
    heads = kv.shape[1]
    columns = weight.shape[2]
    half = columns // 2
    piece = weight.shape[1] // 8
    group, member = lax.axis_index("tm"), lax.axis_index("fsdp")
    row, core = member // 2, member % 2
    beside = group + 1 - 2 * (group % 2)
    along = group + 2 - 4 * ((group // 2) % 2)
    sibling = member + 1 - 2 * core
    opposite = member + 2 - 4 * row
    far = 3 - member
    has_next = jnp.logical_and(member >= 1, group < groups - 1)
    has_previous = jnp.logical_and(member <= 2, group >= 1)

    by_way = 1
    relays = jnp.logical_and(member == 0, group < groups - 1)
    has_relay = jnp.logical_and(member == 1, group >= 1)

    def remote(source, target, send_sem, recv_sem, to_group, to_member):
        return pltpu.make_async_remote_copy(
            src_ref=source,
            dst_ref=target,
            send_sem=send_sem,
            recv_sem=recv_sem,
            device_id=(to_group, to_member),
            device_id_type=pl.DeviceIdType.MESH,
        )

    barrier = pltpu.get_barrier_semaphore()

    def greet(to_group, to_member):
        pl.semaphore_signal(
            barrier, inc=1, device_id=(to_group, to_member), device_id_type=pl.DeviceIdType.MESH
        )

    greet(group, sibling)
    greet(group, opposite)
    greet(beside, member)
    greet(along, member)

    @pl.when(has_next)
    def _():
        greet(group + 1, member - 1)

    @pl.when(has_previous)
    def _():
        greet(group - 1, member + 1)

    @pl.when(relays)
    def _():
        greet(group + 1, 1)

    @pl.when(has_relay)
    def _():
        greet(group - 1, 0)

    load_heads = [
        pltpu.make_async_copy(
            qkv_hbm.at[:, :, pl.ds(h * HEAD, HEAD)], qkv.at[h], local_sem.at[3 + h]
        )
        for h in range(heads)
    ]
    load_weight = pltpu.make_async_copy(weight_hbm, weight.at[member], local_sem.at[0])
    load_latents = pltpu.make_async_copy(latents_hbm, latents, local_sem.at[1])
    load_gates = pltpu.make_async_copy(gates_hbm, gates, local_sem.at[2])
    for load in load_heads:
        load.start()
    load_weight.start()
    load_gates.start()
    load_latents.start()

    peers = 4
    for present in (has_next, has_previous, relays, has_relay):
        peers = peers + present.astype(jnp.int32)
    pl.semaphore_wait(barrier, peers)

    sent = []

    def begin(condition, copy):
        sent.append((condition, copy))
        if condition is None:
            copy.start()
        else:
            pl.when(condition)(copy.start)

    def own_block(h):
        return qkv.at[h, pl.ds(1, 2)]

    def send_opposite(h):
        begin(
            row == 0,
            remote(own_block(h), kv.at[1, h], kv_send.at[0, h], kv_recv.at[1, h], group, opposite),
        )

    def send_near(h):
        direct = has_next
        if h < by_way:
            direct = jnp.logical_and(has_next, member != 2)
            begin(
                jnp.logical_and(has_next, member == 2),
                remote(
                    own_block(h), relay.at[h], relay_send.at[h], relay_recv.at[h], group, opposite
                ),
            )
        begin(
            direct,
            remote(
                own_block(h), kv.at[2, h], kv_send.at[1, h], kv_recv.at[2, h], group + 1, member - 1
            ),
        )
        begin(
            core == 0,
            remote(own_block(h), kv.at[0, h], kv_send.at[2, h], kv_recv.at[0, h], group, sibling),
        )

    def pass_relay(h):
        block = relay.at[h]
        pl.when(relays)(lambda: arrived(block, relay_recv.at[h]))
        begin(
            relays,
            remote(block, kv.at[2, h], relay_pass.at[h], kv_recv.at[2, h], group + 1, member + 1),
        )

    mine = group % 4
    quarters = (
        mine,
        mine + 1 - 2 * (mine % 2),
        mine + 2 - 4 * (mine // 2),
        3 - mine,
    )

    def cut(k):
        return pl.ds(pl.multiple_of((2 * quarters[k // 2] + k % 2) * piece, 16), piece)

    def send_piece(k):
        begin(
            None,
            remote(
                weight_hbm.at[cut(k)],
                weight.at[member, cut(k)],
                w_send.at[k],
                w_recv.at[k],
                group,
                opposite,
            ),
        )

    def send_sibling():
        begin(
            None,
            remote(weight_hbm, weight.at[member], w_send.at[2], w_recv.at[8], group, sibling),
        )

    def arrived(target, sem):
        remote(target, target, w_send.at[0], sem, group, sibling).wait_recv()

    def take_piece(k):
        block = weight.at[opposite, cut(k)]
        arrived(block, w_recv.at[k])

        def pass_on(sem, into, to_group, to_member):
            begin(None, remote(block, block, w_pass.at[sem], w_recv.at[into], to_group, to_member))

        if k < 2:
            pass_on(8 + k, 2 + k, beside, member)
            pass_on(10 + k, 4 + k, along, member)
        if k == 3:
            pass_on(12, 7, along, member)
        if k == 4:
            pass_on(13, 6, beside, member)
        pass_on(k, 9 + k, group, sibling)

    scale = (HEAD ** -0.5) * math.log2(math.e)

    def own_head(index, h):
        return qkv[h, index]

    def scores_of(h, keys):
        return (
            lax.dot_general(
                keys, own_head(0, h), (((1,), (1,)), ((), ())), preferred_element_type=jnp.float32
            )
            * scale
        )

    def mix(values, weights):
        return lax.dot_general(
            values,
            weights.astype(jnp.bfloat16),
            (((0,), (0,)), ((), ())),
            preferred_element_type=jnp.float32,
        )

    def start_head(h):
        scores = scores_of(h, own_head(1, h))
        row_top = jnp.max(scores, axis=0, keepdims=True)
        weights = jnp.exp2(scores - row_top)
        top[h] = row_top
        total[h] = jnp.sum(weights, axis=0, keepdims=True)
        acc[h] = mix(own_head(2, h), weights)

    def add_frame(h, slot):
        scores = scores_of(h, kv[slot, h, 0])
        old_top = top[h]
        row_top = jnp.maximum(old_top, jnp.max(scores, axis=0, keepdims=True))
        weights = jnp.exp2(scores - row_top)
        shrink = jnp.exp2(old_top - row_top)
        top[h] = row_top
        total[h] = total[h] * shrink + jnp.sum(weights, axis=0, keepdims=True)
        acc[h] = acc[h] * shrink + mix(kv[slot, h, 1], weights)

    order = ((3, 1, 3, 1), (1, 3, 2, 2), (2, 2, 1, 3))

    def place_of(j):
        back = by_member(member, order[j])
        return back - 1, jnp.logical_or(group >= 1, member >= back)

    def receive(j, h):
        slot, exists = place_of(j)
        block = kv.at[slot, h]
        pl.when(exists)(lambda: arrived(block, kv_recv.at[slot, h]))
        if j == 0:
            begin(
                jnp.logical_and(exists, member == 2),
                remote(block, kv.at[0, h], kv_pass.at[0, h], kv_recv.at[0, h], group, opposite),
            )
        if j == 1:
            into = by_member(member, (1, 1, 2, 0))
            begin(
                exists,
                remote(
                    block, kv.at[into, h], kv_pass.at[1, h], kv_recv.at[into, h], group, sibling
                ),
            )

    def attend_frame(j, h):
        slot, exists = place_of(j)
        pl.when(exists)(lambda: add_frame(h, slot))

    def finish_head(h):
        attended[:, h * HEAD : (h + 1) * HEAD] = jnp.transpose(acc[h] / total[h]).astype(jnp.bfloat16)

    send_piece(0)
    send_piece(1)
    for h in range(heads):
        load_heads[h].wait()
        send_near(h)
    send_opposite(0)
    send_sibling()

    start_head(0)
    start_head(1)
    receive(0, 0)
    take_piece(0)
    for h in range(1, heads - 1):
        send_opposite(h)
    start_head(2)
    receive(0, 1)
    take_piece(1)
    send_opposite(heads - 1)
    for h in range(3, heads):
        start_head(h)
    for h in range(by_way):
        pass_relay(h)
    take_piece(2)
    take_piece(4)
    for h in range(2, heads):
        receive(0, h)
    attend_frame(0, 0)
    take_piece(3)
    take_piece(5)
    receive(1, 0)
    attend_frame(0, 1)
    take_piece(6)
    take_piece(7)
    receive(1, 1)
    for h in range(2, heads):
        attend_frame(0, h)
    load_gates.wait()
    step_index = lax.broadcasted_iota(jnp.int32, gates.shape, 0)
    gate_row[...] = jnp.sum(
        jnp.where(step_index == steps_ref[member], gates[...], 0.0), axis=0, keepdims=True
    )
    for h in range(heads):
        if h >= 2:
            receive(1, h)
        if h >= 1:
            receive(2, h - 1)
        attend_frame(1, h)
        if h >= 1:
            attend_frame(2, h - 1)
            finish_head(h - 1)
    done = (heads - 1) * HEAD
    early = (member, sibling, opposite)
    load_weight.wait()
    load_latents.wait()
    arrived(weight.at[sibling], w_recv.at[8])
    for i, owner in enumerate(early):
        for start in (0, half):
            partial[i, :, start : start + half] = jnp.dot(
                attended[:, :done],
                weight[owner, :done, start : start + half],
                preferred_element_type=jnp.float32,
            )

    receive(2, heads - 1)
    attend_frame(2, heads - 1)
    finish_head(heads - 1)

    def update(owner, start, branch):
        place = pl.ds(pl.multiple_of(owner * columns + start, 128), half)
        out[:, place] = (
            latents[:, place].astype(jnp.float32) + gate_row[:, place] * branch
        ).astype(jnp.bfloat16)

    for i, owner in enumerate(early):
        for start in (0, half):
            branch = partial[i, :, start : start + half] + jnp.dot(
                attended[:, done:],
                weight[owner, done:, start : start + half],
                preferred_element_type=jnp.float32,
            )
            update(owner, start, branch)
    for k in range(8):
        arrived(weight.at[far, cut(k)], w_recv.at[9 + k])
    for start in (0, half):
        branch = jnp.dot(
            attended[...],
            weight[far, :, start : start + half],
            preferred_element_type=jnp.float32,
        )
        update(far, start, branch)

    for condition, copy in sent:
        if condition is None:
            copy.wait_send()
        else:
            pl.when(condition)(copy.wait_send)


def frame_body(latents, projected, out_weight, gate_table, timesteps, groups):
    rows, width = latents.shape
    inner, columns = out_weight.shape
    heads = inner // HEAD
    qkv = projected.transpose(1, 0, 2)
    in_hbm = pl.BlockSpec(memory_space=pltpu.HBM)
    return pl.pallas_call(
        functools.partial(frame_kernel, groups),
        out_shape=pltpu.VMEM((rows, width), jnp.bfloat16),
        in_specs=[pl.BlockSpec(memory_space=pltpu.SMEM)] + [in_hbm] * 4,
        out_specs=pl.BlockSpec(memory_space=pltpu.VMEM),
        scratch_shapes=[
            pltpu.VMEM((heads, 3, rows, HEAD), jnp.bfloat16),
            pltpu.VMEM((3, heads, 2, rows, HEAD), jnp.bfloat16),
            pltpu.VMEM((1, 2, rows, HEAD), jnp.bfloat16),
            pltpu.VMEM((4, inner, columns), jnp.bfloat16),
            pltpu.VMEM((rows, width), jnp.bfloat16),
            pltpu.VMEM(gate_table.shape, jnp.float32),
            pltpu.VMEM((1, width), jnp.float32),
            pltpu.VMEM((heads, 1, rows), jnp.float32),
            pltpu.VMEM((heads, 1, rows), jnp.float32),
            pltpu.VMEM((heads, HEAD, rows), jnp.float32),
            pltpu.VMEM((rows, inner), jnp.bfloat16),
            pltpu.VMEM((3, rows, columns), jnp.float32),
            pltpu.SemaphoreType.DMA((3 + heads,)),
            pltpu.SemaphoreType.DMA((3, heads)),
            pltpu.SemaphoreType.DMA((2, heads)),
            pltpu.SemaphoreType.DMA((3, heads)),
            pltpu.SemaphoreType.DMA((3,)),
            pltpu.SemaphoreType.DMA((14,)),
            pltpu.SemaphoreType.DMA((17,)),
            pltpu.SemaphoreType.DMA((1,)),
            pltpu.SemaphoreType.DMA((1,)),
            pltpu.SemaphoreType.DMA((1,)),
        ],
        compiler_params=pltpu.CompilerParams(
            collective_id=0, has_side_effects=True, vmem_limit_bytes=56 * 1024 * 1024
        ),
        cost_estimate=pl.CostEstimate(
            flops=2 * rows * inner * (8 * rows + width),
            bytes_accessed=4 * rows * width + 2 * inner * width,
            transcendentals=4 * heads * rows * rows,
        ),
    )(timesteps, latents, qkv, out_weight, gate_table)


def solution(mesh):
    in_specs = (
        P(("tm", "fsdp"), None),
        P(("tm", "fsdp"), None, None),
        P(None, "fsdp"),
        P(),
        P("tm"),
    )
    out_specs = P(("tm", "fsdp"), None)
    groups, members = mesh.shape["tm"], mesh.shape["fsdp"]

    def local(latents, projected, out_weight, gate_table, timesteps):
        one_frame_each = latents.shape[0] == FRAME_TOK and timesteps.shape[0] == members
        if one_frame_each and members == 4 and groups % 4 == 0:
            return frame_body(latents, projected, out_weight, gate_table, timesteps, groups)
        return body(latents, projected, out_weight, gate_table, timesteps)

    return jax.shard_map(local, mesh=mesh, in_specs=in_specs, out_specs=out_specs, check_vma=False)
```

```python
import functools
import math

import jax
import jax.numpy as jnp
from jax import lax
from jax.experimental import pallas as pl
from jax.experimental.pallas import tpu as pltpu
from jax.sharding import PartitionSpec as P

FRAME_TOK = 256


def passed_along(value, axis, steps):
    count = lax.axis_size(axis)
    initial, last = (max(0, -steps), min(count, count - steps))
    return lax.ppermute(value, axis, [(source, source + steps) for source in range(initial, last)])


def attend(queries, extended, first_frame, frame_count):
    pair_rows = 2 * FRAME_TOK
    key_count = 5 * FRAME_TOK
    score_scale = queries.shape[1] ** (-0.5)
    row_frame = jnp.arange(pair_rows, dtype=jnp.int32) // FRAME_TOK
    col_frame = jnp.arange(key_count, dtype=jnp.int32) // FRAME_TOK

    def frame_pair(pair_index):
        offset = pair_index * pair_rows
        query_block = lax.dynamic_slice_in_dim(queries, offset, pair_rows, 0)
        window = lax.dynamic_slice_in_dim(extended, offset, key_count, 0)
        key_block = window[:, 0]
        value_block = window[:, 1]
        scores = (
            lax.dot_general(
                query_block, key_block, (((1,), (1,)), ((), ())), preferred_element_type=jnp.float32
            )
            * score_scale
        )
        distance = col_frame[None, :] - row_frame[:, None]
        existing = first_frame + 2 * pair_index + col_frame - 3 >= 0
        allowed = (distance >= 0) & (distance <= 3) & existing[None, :]
        scores = jnp.where(allowed, scores, -1e30)
        row_max = jnp.max(scores, axis=-1, keepdims=True)
        weights = jnp.exp(scores - row_max)
        row_sum = jnp.sum(weights, axis=-1, keepdims=True)
        probability = (weights / row_sum).astype(jnp.bfloat16)
        return jnp.dot(probability, value_block, preferred_element_type=jnp.float32).astype(
            jnp.bfloat16
        )

    blocks = lax.map(frame_pair, jnp.arange(frame_count // 2, dtype=jnp.int32))
    return blocks.reshape(frame_count * FRAME_TOK, queries.shape[1])


def body(latents, projected, out_weight, gate_table, timesteps):
    row_count = latents.shape[0]
    frame_count = timesteps.shape[0]
    group_tokens = frame_count * FRAME_TOK
    head_view = lax.all_to_all(projected, "fsdp", split_axis=2, concat_axis=0, tiled=True)
    queries = head_view[:, 0]
    key_values = head_view[:, 1:3]
    trailing = passed_along(key_values[group_tokens - 3 * FRAME_TOK :], "tm", 1)
    extended = jnp.concatenate([trailing, key_values], axis=0)
    first_frame = lax.axis_index("tm") * frame_count
    attended = attend(queries, extended, first_frame, frame_count)
    gathered_heads = lax.all_to_all(attended, "fsdp", split_axis=0, concat_axis=1, tiled=True)
    update = jnp.dot(
        gathered_heads,
        lax.all_gather(out_weight, "fsdp", axis=1, tiled=True),
        preferred_element_type=jnp.float32,
    )
    step_count = gate_table.shape[0]
    step_onehot = (timesteps[:, None] == jnp.arange(step_count, dtype=jnp.int32)[None, :]).astype(
        jnp.float32
    )
    frame_gates = jnp.dot(step_onehot, gate_table, precision=lax.Precision.HIGHEST)
    row_frame = (
        lax.axis_index("fsdp") * row_count + jnp.arange(row_count, dtype=jnp.int32)
    ) // FRAME_TOK
    row_onehot = (row_frame[:, None] == jnp.arange(frame_count, dtype=jnp.int32)[None, :]).astype(
        jnp.float32
    )
    row_gates = jnp.dot(row_onehot, frame_gates, precision=lax.Precision.HIGHEST)
    return (latents.astype(jnp.float32) + row_gates * update).astype(jnp.bfloat16)


HEAD = 128


def by_member(member, values):
    row, core = member // 2, member % 2
    v0, v1, v2, v3 = values
    return v0 + (v1 - v0) * core + (v2 - v0) * row + (v3 - v2 - v1 + v0) * core * row


def frame_kernel(
    groups,
    steps_ref,
    latents_hbm,
    qkv_hbm,
    weight_hbm,
    gates_hbm,
    out,
    qkv,
    kv,
    weight,
    latents,
    gates,
    gate_row,
    top,
    total,
    acc,
    attended,
    local_sem,
    kv_send,
    kv_pass,
    kv_recv,
    w_send,
    w_pass,
    w_recv,
):
    heads = kv.shape[1]
    columns = weight.shape[2]
    half = columns // 2
    piece = weight.shape[1] // 8
    group, member = lax.axis_index("tm"), lax.axis_index("fsdp")
    row, core = member // 2, member % 2
    across = group + 1 - 2 * (group % 2)
    sibling = member + 1 - 2 * core
    opposite = member + 2 - 4 * row
    far = 3 - member
    has_next = jnp.logical_and(member >= 1, group < groups - 1)
    has_previous = jnp.logical_and(member <= 2, group >= 1)

    def remote(source, target, send_sem, recv_sem, to_group, to_member):
        return pltpu.make_async_remote_copy(
            src_ref=source,
            dst_ref=target,
            send_sem=send_sem,
            recv_sem=recv_sem,
            device_id=(to_group, to_member),
            device_id_type=pl.DeviceIdType.MESH,
        )

    barrier = pltpu.get_barrier_semaphore()

    def greet(to_group, to_member):
        pl.semaphore_signal(
            barrier, inc=1, device_id=(to_group, to_member), device_id_type=pl.DeviceIdType.MESH
        )

    greet(group, sibling)
    greet(group, opposite)
    greet(across, member)

    @pl.when(has_next)
    def _():
        greet(group + 1, member - 1)

    @pl.when(has_previous)
    def _():
        greet(group - 1, member + 1)

    load_heads = [
        pltpu.make_async_copy(
            qkv_hbm.at[:, :, pl.ds(h * HEAD, HEAD)], qkv.at[h], local_sem.at[3 + h]
        )
        for h in range(heads)
    ]
    load_weight = pltpu.make_async_copy(weight_hbm, weight.at[member], local_sem.at[0])
    load_latents = pltpu.make_async_copy(latents_hbm, latents, local_sem.at[1])
    load_gates = pltpu.make_async_copy(gates_hbm, gates, local_sem.at[2])
    for load in load_heads:
        load.start()
    load_weight.start()
    load_gates.start()
    load_latents.start()

    pl.semaphore_wait(barrier, 3 + has_next.astype(jnp.int32) + has_previous.astype(jnp.int32))

    sent = []

    def begin(condition, copy):
        sent.append((condition, copy))
        if condition is None:
            copy.start()
        else:
            pl.when(condition)(copy.start)

    def own_block(h):
        return qkv.at[h, pl.ds(1, 2)]

    def send_opposite(h):
        begin(
            row == 0,
            remote(own_block(h), kv.at[1, h], kv_send.at[0, h], kv_recv.at[1, h], group, opposite),
        )

    def send_near(h):
        begin(
            has_next,
            remote(
                own_block(h), kv.at[2, h], kv_send.at[1, h], kv_recv.at[2, h], group + 1, member - 1
            ),
        )
        begin(
            core == 0,
            remote(own_block(h), kv.at[0, h], kv_send.at[2, h], kv_recv.at[0, h], group, sibling),
        )

    def cut(k):
        part = group % 2 if k < 4 else 1 - group % 2
        return pl.ds(pl.multiple_of((4 * part + k % 4) * piece, 16), piece)

    def send_piece(k):
        begin(
            None,
            remote(
                weight_hbm.at[cut(k)],
                weight.at[member, cut(k)],
                w_send.at[k],
                w_recv.at[k],
                group,
                opposite,
            ),
        )

    def send_sibling():
        begin(
            None,
            remote(weight_hbm, weight.at[member], w_send.at[4], w_recv.at[8], group, sibling),
        )

    def arrived(target, sem):
        remote(target, target, w_send.at[0], sem, group, sibling).wait_recv()

    def take_piece(k):
        block = weight.at[opposite, cut(k)]
        arrived(block, w_recv.at[k])
        if k < 4:
            begin(
                None,
                remote(block, block, w_pass.at[8 + k], w_recv.at[4 + k], across, member),
            )
        begin(
            None,
            remote(block, block, w_pass.at[k], w_recv.at[9 + k], group, sibling),
        )

    scale = (HEAD ** -0.5) * math.log2(math.e)

    def own_head(index, h):
        return qkv[h, index]

    def scores_of(h, keys):
        return (
            lax.dot_general(
                keys, own_head(0, h), (((1,), (1,)), ((), ())), preferred_element_type=jnp.float32
            )
            * scale
        )

    def mix(values, weights):
        return lax.dot_general(
            values,
            weights.astype(jnp.bfloat16),
            (((0,), (0,)), ((), ())),
            preferred_element_type=jnp.float32,
        )

    def start_head(h):
        scores = scores_of(h, own_head(1, h))
        row_top = jnp.max(scores, axis=0, keepdims=True)
        weights = jnp.exp2(scores - row_top)
        top[h] = row_top
        total[h] = jnp.sum(weights, axis=0, keepdims=True)
        acc[h] = mix(own_head(2, h), weights)

    def add_frame(h, slot):
        scores = scores_of(h, kv[slot, h, 0])
        old_top = top[h]
        row_top = jnp.maximum(old_top, jnp.max(scores, axis=0, keepdims=True))
        weights = jnp.exp2(scores - row_top)
        shrink = jnp.exp2(old_top - row_top)
        top[h] = row_top
        total[h] = total[h] * shrink + jnp.sum(weights, axis=0, keepdims=True)
        acc[h] = acc[h] * shrink + mix(kv[slot, h, 1], weights)

    order = ((3, 1, 3, 1), (1, 3, 2, 2), (2, 2, 1, 3))

    def place_of(j):
        back = by_member(member, order[j])
        return back - 1, jnp.logical_or(group >= 1, member >= back)

    def receive(j, h):
        slot, exists = place_of(j)
        block = kv.at[slot, h]
        pl.when(exists)(lambda: arrived(block, kv_recv.at[slot, h]))
        if j == 0:
            begin(
                jnp.logical_and(exists, member == 2),
                remote(block, kv.at[0, h], kv_pass.at[0, h], kv_recv.at[0, h], group, opposite),
            )
        if j == 1:
            into = by_member(member, (1, 1, 2, 0))
            begin(
                exists,
                remote(
                    block, kv.at[into, h], kv_pass.at[1, h], kv_recv.at[into, h], group, sibling
                ),
            )

    def attend_frame(j, h):
        slot, exists = place_of(j)
        pl.when(exists)(lambda: add_frame(h, slot))

    def finish_head(h):
        attended[:, h * HEAD : (h + 1) * HEAD] = jnp.transpose(acc[h] / total[h]).astype(jnp.bfloat16)

    for k in range(4):
        send_piece(k)
    for h in range(heads):
        load_heads[h].wait()
        send_near(h)
    send_opposite(0)
    send_sibling()

    start_head(0)
    start_head(1)
    receive(0, 0)
    take_piece(0)
    receive(0, 1)
    send_opposite(1)
    for h in range(2, heads):
        start_head(h)
        receive(0, h)
    attend_frame(0, 0)
    take_piece(1)
    send_opposite(2)
    attend_frame(0, 1)
    take_piece(2)
    for h in range(3, heads):
        send_opposite(h)
    attend_frame(0, 2)
    take_piece(3)
    for h in range(3, heads):
        attend_frame(0, h)
    load_gates.wait()
    step_index = lax.broadcasted_iota(jnp.int32, gates.shape, 0)
    gate_row[...] = jnp.sum(
        jnp.where(step_index == steps_ref[member], gates[...], 0.0), axis=0, keepdims=True
    )
    for h in range(heads):
        receive(1, h)
        if h < 4:
            take_piece(4 + h)
        if h >= 1:
            receive(2, h - 1)
        attend_frame(1, h)
        if h >= 1:
            attend_frame(2, h - 1)
            finish_head(h - 1)
    receive(2, heads - 1)
    attend_frame(2, heads - 1)
    finish_head(heads - 1)

    def project(owner, start, width):
        place = pl.ds(pl.multiple_of(owner * columns + start, 128), width)
        branch = jnp.dot(
            attended[...],
            weight[owner, :, pl.ds(start, width)],
            preferred_element_type=jnp.float32,
        )
        out[:, place] = (
            latents[:, place].astype(jnp.float32) + gate_row[:, place] * branch
        ).astype(jnp.bfloat16)

    load_weight.wait()
    load_latents.wait()
    project(member, 0, half)
    project(member, half, half)
    arrived(weight.at[sibling], w_recv.at[8])
    project(sibling, 0, half)
    project(sibling, half, half)
    project(opposite, 0, half)
    project(opposite, half, half)
    for k in range(8):
        arrived(weight.at[far, cut(k)], w_recv.at[9 + k])
    project(far, 0, half)
    project(far, half, half)

    for condition, copy in sent:
        if condition is None:
            copy.wait_send()
        else:
            pl.when(condition)(copy.wait_send)


def frame_body(latents, projected, out_weight, gate_table, timesteps, groups):
    rows, width = latents.shape
    inner, columns = out_weight.shape
    heads = inner // HEAD
    qkv = projected.transpose(1, 0, 2)
    in_hbm = pl.BlockSpec(memory_space=pltpu.HBM)
    return pl.pallas_call(
        functools.partial(frame_kernel, groups),
        out_shape=pltpu.VMEM((rows, width), jnp.bfloat16),
        in_specs=[pl.BlockSpec(memory_space=pltpu.SMEM)] + [in_hbm] * 4,
        out_specs=pl.BlockSpec(memory_space=pltpu.VMEM),
        scratch_shapes=[
            pltpu.VMEM((heads, 3, rows, HEAD), jnp.bfloat16),
            pltpu.VMEM((3, heads, 2, rows, HEAD), jnp.bfloat16),
            pltpu.VMEM((4, inner, columns), jnp.bfloat16),
            pltpu.VMEM((rows, width), jnp.bfloat16),
            pltpu.VMEM(gate_table.shape, jnp.float32),
            pltpu.VMEM((1, width), jnp.float32),
            pltpu.VMEM((heads, 1, rows), jnp.float32),
            pltpu.VMEM((heads, 1, rows), jnp.float32),
            pltpu.VMEM((heads, HEAD, rows), jnp.float32),
            pltpu.VMEM((rows, inner), jnp.bfloat16),
            pltpu.SemaphoreType.DMA((3 + heads,)),
            pltpu.SemaphoreType.DMA((3, heads)),
            pltpu.SemaphoreType.DMA((2, heads)),
            pltpu.SemaphoreType.DMA((3, heads)),
            pltpu.SemaphoreType.DMA((5,)),
            pltpu.SemaphoreType.DMA((12,)),
            pltpu.SemaphoreType.DMA((17,)),
        ],
        compiler_params=pltpu.CompilerParams(
            collective_id=0, has_side_effects=True, vmem_limit_bytes=56 * 1024 * 1024
        ),
        cost_estimate=pl.CostEstimate(
            flops=2 * rows * inner * (8 * rows + width),
            bytes_accessed=4 * rows * width + 2 * inner * width,
            transcendentals=4 * heads * rows * rows,
        ),
    )(timesteps, latents, qkv, out_weight, gate_table)


def solution(mesh):
    in_specs = (
        P(("tm", "fsdp"), None),
        P(("tm", "fsdp"), None, None),
        P(None, "fsdp"),
        P(),
        P("tm"),
    )
    out_specs = P(("tm", "fsdp"), None)
    groups, members = mesh.shape["tm"], mesh.shape["fsdp"]

    def local(latents, projected, out_weight, gate_table, timesteps):
        one_frame_each = latents.shape[0] == FRAME_TOK and timesteps.shape[0] == members
        if one_frame_each and members == 4 and groups % 2 == 0:
            return frame_body(latents, projected, out_weight, gate_table, timesteps, groups)
        return body(latents, projected, out_weight, gate_table, timesteps)

    return jax.shard_map(local, mesh=mesh, in_specs=in_specs, out_specs=out_specs, check_vma=False)
```

```python
import functools
import math

import jax
import jax.numpy as jnp
from jax import lax
from jax.experimental import pallas as pl
from jax.experimental.pallas import tpu as pltpu
from jax.sharding import PartitionSpec as P

FRAME_TOK = 256


def passed_along(value, axis, steps):
    count = lax.axis_size(axis)
    initial, last = (max(0, -steps), min(count, count - steps))
    return lax.ppermute(value, axis, [(source, source + steps) for source in range(initial, last)])


def attend(queries, extended, first_frame, frame_count):
    pair_rows = 2 * FRAME_TOK
    key_count = 5 * FRAME_TOK
    score_scale = queries.shape[1] ** (-0.5)
    row_frame = jnp.arange(pair_rows, dtype=jnp.int32) // FRAME_TOK
    col_frame = jnp.arange(key_count, dtype=jnp.int32) // FRAME_TOK

    def frame_pair(pair_index):
        offset = pair_index * pair_rows
        query_block = lax.dynamic_slice_in_dim(queries, offset, pair_rows, 0)
        window = lax.dynamic_slice_in_dim(extended, offset, key_count, 0)
        key_block = window[:, 0]
        value_block = window[:, 1]
        scores = (
            lax.dot_general(
                query_block, key_block, (((1,), (1,)), ((), ())), preferred_element_type=jnp.float32
            )
            * score_scale
        )
        distance = col_frame[None, :] - row_frame[:, None]
        existing = first_frame + 2 * pair_index + col_frame - 3 >= 0
        allowed = (distance >= 0) & (distance <= 3) & existing[None, :]
        scores = jnp.where(allowed, scores, -1e30)
        row_max = jnp.max(scores, axis=-1, keepdims=True)
        weights = jnp.exp(scores - row_max)
        row_sum = jnp.sum(weights, axis=-1, keepdims=True)
        probability = (weights / row_sum).astype(jnp.bfloat16)
        return jnp.dot(probability, value_block, preferred_element_type=jnp.float32).astype(
            jnp.bfloat16
        )

    blocks = lax.map(frame_pair, jnp.arange(frame_count // 2, dtype=jnp.int32))
    return blocks.reshape(frame_count * FRAME_TOK, queries.shape[1])


def body(latents, projected, out_weight, gate_table, timesteps):
    row_count = latents.shape[0]
    frame_count = timesteps.shape[0]
    group_tokens = frame_count * FRAME_TOK
    head_view = lax.all_to_all(projected, "fsdp", split_axis=2, concat_axis=0, tiled=True)
    queries = head_view[:, 0]
    key_values = head_view[:, 1:3]
    trailing = passed_along(key_values[group_tokens - 3 * FRAME_TOK :], "tm", 1)
    extended = jnp.concatenate([trailing, key_values], axis=0)
    first_frame = lax.axis_index("tm") * frame_count
    attended = attend(queries, extended, first_frame, frame_count)
    gathered_heads = lax.all_to_all(attended, "fsdp", split_axis=0, concat_axis=1, tiled=True)
    update = jnp.dot(
        gathered_heads,
        lax.all_gather(out_weight, "fsdp", axis=1, tiled=True),
        preferred_element_type=jnp.float32,
    )
    step_count = gate_table.shape[0]
    step_onehot = (timesteps[:, None] == jnp.arange(step_count, dtype=jnp.int32)[None, :]).astype(
        jnp.float32
    )
    frame_gates = jnp.dot(step_onehot, gate_table, precision=lax.Precision.HIGHEST)
    row_frame = (
        lax.axis_index("fsdp") * row_count + jnp.arange(row_count, dtype=jnp.int32)
    ) // FRAME_TOK
    row_onehot = (row_frame[:, None] == jnp.arange(frame_count, dtype=jnp.int32)[None, :]).astype(
        jnp.float32
    )
    row_gates = jnp.dot(row_onehot, frame_gates, precision=lax.Precision.HIGHEST)
    return (latents.astype(jnp.float32) + row_gates * update).astype(jnp.bfloat16)


HEAD = 128


def by_member(member, values):
    row, core = member // 2, member % 2
    v0, v1, v2, v3 = values
    return v0 + (v1 - v0) * core + (v2 - v0) * row + (v3 - v2 - v1 + v0) * core * row


def frame_kernel(
    groups,
    steps_ref,
    latents_hbm,
    qkv_hbm,
    weight_hbm,
    gates_hbm,
    out,
    qkv,
    kv,
    weight,
    latents,
    gates,
    gate_row,
    top,
    total,
    acc,
    attended,
    local_sem,
    kv_send,
    kv_pass,
    kv_recv,
    w_send,
    w_pass,
    w_recv,
):
    heads = kv.shape[1]
    columns = weight.shape[2]
    half = columns // 2
    piece = weight.shape[1] // 8
    group, member = lax.axis_index("tm"), lax.axis_index("fsdp")
    row, core = member // 2, member % 2
    across = group + 1 - 2 * (group % 2)
    sibling = member + 1 - 2 * core
    opposite = member + 2 - 4 * row
    far = 3 - member
    has_next = jnp.logical_and(member >= 1, group < groups - 1)
    has_previous = jnp.logical_and(member <= 2, group >= 1)

    def remote(source, target, send_sem, recv_sem, to_group, to_member):
        return pltpu.make_async_remote_copy(
            src_ref=source,
            dst_ref=target,
            send_sem=send_sem,
            recv_sem=recv_sem,
            device_id=(to_group, to_member),
            device_id_type=pl.DeviceIdType.MESH,
        )

    barrier = pltpu.get_barrier_semaphore()

    def greet(to_group, to_member):
        pl.semaphore_signal(
            barrier, inc=1, device_id=(to_group, to_member), device_id_type=pl.DeviceIdType.MESH
        )

    greet(group, sibling)
    greet(group, opposite)
    greet(across, member)

    @pl.when(has_next)
    def _():
        greet(group + 1, member - 1)

    @pl.when(has_previous)
    def _():
        greet(group - 1, member + 1)

    load_heads = [
        pltpu.make_async_copy(
            qkv_hbm.at[:, :, pl.ds(h * HEAD, HEAD)], qkv.at[h], local_sem.at[3 + h]
        )
        for h in range(heads)
    ]
    load_weight = pltpu.make_async_copy(weight_hbm, weight.at[member], local_sem.at[0])
    load_latents = pltpu.make_async_copy(latents_hbm, latents, local_sem.at[1])
    load_gates = pltpu.make_async_copy(gates_hbm, gates, local_sem.at[2])
    for load in load_heads:
        load.start()
    load_weight.start()
    load_gates.start()
    load_latents.start()

    pl.semaphore_wait(barrier, 3 + has_next.astype(jnp.int32) + has_previous.astype(jnp.int32))

    sent = []

    def begin(condition, copy):
        sent.append((condition, copy))
        if condition is None:
            copy.start()
        else:
            pl.when(condition)(copy.start)

    def own_block(h):
        return qkv.at[h, pl.ds(1, 2)]

    def send_opposite(h):
        begin(
            row == 0,
            remote(own_block(h), kv.at[1, h], kv_send.at[0, h], kv_recv.at[1, h], group, opposite),
        )

    def send_near(h):
        begin(
            has_next,
            remote(
                own_block(h), kv.at[2, h], kv_send.at[1, h], kv_recv.at[2, h], group + 1, member - 1
            ),
        )
        begin(
            core == 0,
            remote(own_block(h), kv.at[0, h], kv_send.at[2, h], kv_recv.at[0, h], group, sibling),
        )

    def cut(k):
        part = group % 2 if k < 4 else 1 - group % 2
        return pl.ds(pl.multiple_of((4 * part + k % 4) * piece, 16), piece)

    def send_piece(k):
        begin(
            None,
            remote(
                weight_hbm.at[cut(k)],
                weight.at[member, cut(k)],
                w_send.at[k],
                w_recv.at[k],
                group,
                opposite,
            ),
        )

    def send_sibling():
        begin(
            None,
            remote(weight_hbm, weight.at[member], w_send.at[4], w_recv.at[8], group, sibling),
        )

    def arrived(target, sem):
        remote(target, target, w_send.at[0], sem, group, sibling).wait_recv()

    def take_piece(k):
        block = weight.at[opposite, cut(k)]
        arrived(block, w_recv.at[k])
        if k < 4:
            begin(
                None,
                remote(block, block, w_pass.at[8 + k], w_recv.at[4 + k], across, member),
            )
        begin(
            None,
            remote(block, block, w_pass.at[k], w_recv.at[9 + k], group, sibling),
        )

    scale = (HEAD ** -0.5) * math.log2(math.e)

    def own_head(index, h):
        return qkv[h, index]

    def scores_of(h, keys):
        return (
            lax.dot_general(
                keys, own_head(0, h), (((1,), (1,)), ((), ())), preferred_element_type=jnp.float32
            )
            * scale
        )

    def mix(values, weights):
        return lax.dot_general(
            values,
            weights.astype(jnp.bfloat16),
            (((0,), (0,)), ((), ())),
            preferred_element_type=jnp.float32,
        )

    def start_head(h):
        scores = scores_of(h, own_head(1, h))
        row_top = jnp.max(scores, axis=0, keepdims=True)
        weights = jnp.exp2(scores - row_top)
        top[h] = row_top
        total[h] = jnp.sum(weights, axis=0, keepdims=True)
        acc[h] = mix(own_head(2, h), weights)

    def add_frame(h, slot):
        scores = scores_of(h, kv[slot, h, 0])
        old_top = top[h]
        row_top = jnp.maximum(old_top, jnp.max(scores, axis=0, keepdims=True))
        weights = jnp.exp2(scores - row_top)
        shrink = jnp.exp2(old_top - row_top)
        top[h] = row_top
        total[h] = total[h] * shrink + jnp.sum(weights, axis=0, keepdims=True)
        acc[h] = acc[h] * shrink + mix(kv[slot, h, 1], weights)

    order = ((3, 1, 3, 1), (1, 3, 2, 2), (2, 2, 1, 3))

    def place_of(j):
        back = by_member(member, order[j])
        return back - 1, jnp.logical_or(group >= 1, member >= back)

    def receive(j, h):
        slot, exists = place_of(j)
        block = kv.at[slot, h]
        pl.when(exists)(lambda: arrived(block, kv_recv.at[slot, h]))
        if j == 0:
            begin(
                jnp.logical_and(exists, member == 2),
                remote(block, kv.at[0, h], kv_pass.at[0, h], kv_recv.at[0, h], group, opposite),
            )
        if j == 1:
            into = by_member(member, (1, 1, 2, 0))
            begin(
                exists,
                remote(
                    block, kv.at[into, h], kv_pass.at[1, h], kv_recv.at[into, h], group, sibling
                ),
            )

    def attend_frame(j, h):
        slot, exists = place_of(j)
        pl.when(exists)(lambda: add_frame(h, slot))

    def finish_head(h):
        attended[:, h * HEAD : (h + 1) * HEAD] = jnp.transpose(acc[h] / total[h]).astype(jnp.bfloat16)

    for k in range(4):
        send_piece(k)
    for h in range(heads):
        load_heads[h].wait()
        send_near(h)
    send_opposite(0)
    send_opposite(1)
    send_sibling()

    start_head(0)
    start_head(1)
    receive(0, 0)
    take_piece(0)
    receive(0, 1)
    send_opposite(2)
    for h in range(2, heads):
        start_head(h)
        receive(0, h)
    attend_frame(0, 0)
    take_piece(1)
    for h in range(3, heads):
        send_opposite(h)
    attend_frame(0, 1)
    take_piece(2)
    attend_frame(0, 2)
    take_piece(3)
    for h in range(3, heads):
        attend_frame(0, h)
    load_gates.wait()
    step_index = lax.broadcasted_iota(jnp.int32, gates.shape, 0)
    gate_row[...] = jnp.sum(
        jnp.where(step_index == steps_ref[member], gates[...], 0.0), axis=0, keepdims=True
    )
    for h in range(heads):
        if h < 4:
            take_piece(4 + h)
        receive(1, h)
        if h >= 1:
            receive(2, h - 1)
        attend_frame(1, h)
        if h >= 1:
            attend_frame(2, h - 1)
            finish_head(h - 1)
    receive(2, heads - 1)
    attend_frame(2, heads - 1)
    finish_head(heads - 1)

    def project(owner, start, width):
        place = pl.ds(pl.multiple_of(owner * columns + start, 128), width)
        branch = jnp.dot(
            attended[...],
            weight[owner, :, pl.ds(start, width)],
            preferred_element_type=jnp.float32,
        )
        out[:, place] = (
            latents[:, place].astype(jnp.float32) + gate_row[:, place] * branch
        ).astype(jnp.bfloat16)

    load_weight.wait()
    load_latents.wait()
    project(member, 0, half)
    project(member, half, half)
    arrived(weight.at[sibling], w_recv.at[8])
    project(sibling, 0, half)
    project(sibling, half, half)
    project(opposite, 0, half)
    project(opposite, half, half)
    for k in range(8):
        arrived(weight.at[far, cut(k)], w_recv.at[9 + k])
    project(far, 0, half)
    project(far, half, half)

    for condition, copy in sent:
        if condition is None:
            copy.wait_send()
        else:
            pl.when(condition)(copy.wait_send)


def frame_body(latents, projected, out_weight, gate_table, timesteps, groups):
    rows, width = latents.shape
    inner, columns = out_weight.shape
    heads = inner // HEAD
    qkv = projected.transpose(1, 0, 2)
    in_hbm = pl.BlockSpec(memory_space=pltpu.HBM)
    return pl.pallas_call(
        functools.partial(frame_kernel, groups),
        out_shape=pltpu.VMEM((rows, width), jnp.bfloat16),
        in_specs=[pl.BlockSpec(memory_space=pltpu.SMEM)] + [in_hbm] * 4,
        out_specs=pl.BlockSpec(memory_space=pltpu.VMEM),
        scratch_shapes=[
            pltpu.VMEM((heads, 3, rows, HEAD), jnp.bfloat16),
            pltpu.VMEM((3, heads, 2, rows, HEAD), jnp.bfloat16),
            pltpu.VMEM((4, inner, columns), jnp.bfloat16),
            pltpu.VMEM((rows, width), jnp.bfloat16),
            pltpu.VMEM(gate_table.shape, jnp.float32),
            pltpu.VMEM((1, width), jnp.float32),
            pltpu.VMEM((heads, 1, rows), jnp.float32),
            pltpu.VMEM((heads, 1, rows), jnp.float32),
            pltpu.VMEM((heads, HEAD, rows), jnp.float32),
            pltpu.VMEM((rows, inner), jnp.bfloat16),
            pltpu.SemaphoreType.DMA((3 + heads,)),
            pltpu.SemaphoreType.DMA((3, heads)),
            pltpu.SemaphoreType.DMA((2, heads)),
            pltpu.SemaphoreType.DMA((3, heads)),
            pltpu.SemaphoreType.DMA((5,)),
            pltpu.SemaphoreType.DMA((12,)),
            pltpu.SemaphoreType.DMA((17,)),
        ],
        compiler_params=pltpu.CompilerParams(
            collective_id=0, has_side_effects=True, vmem_limit_bytes=56 * 1024 * 1024
        ),
        cost_estimate=pl.CostEstimate(
            flops=2 * rows * inner * (8 * rows + width),
            bytes_accessed=4 * rows * width + 2 * inner * width,
            transcendentals=4 * heads * rows * rows,
        ),
    )(timesteps, latents, qkv, out_weight, gate_table)


def solution(mesh):
    in_specs = (
        P(("tm", "fsdp"), None),
        P(("tm", "fsdp"), None, None),
        P(None, "fsdp"),
        P(),
        P("tm"),
    )
    out_specs = P(("tm", "fsdp"), None)
    groups, members = mesh.shape["tm"], mesh.shape["fsdp"]

    def local(latents, projected, out_weight, gate_table, timesteps):
        one_frame_each = latents.shape[0] == FRAME_TOK and timesteps.shape[0] == members
        if one_frame_each and members == 4 and groups % 2 == 0:
            return frame_body(latents, projected, out_weight, gate_table, timesteps, groups)
        return body(latents, projected, out_weight, gate_table, timesteps)

    return jax.shard_map(local, mesh=mesh, in_specs=in_specs, out_specs=out_specs, check_vma=False)
```
